128 devices in a mesh: sector: 4 (over y_hi, core), ops: 32 (over x, z, y_lo).
Axes of the slice: x: 4, y: 4 (y_hi: 2, y_lo: 2; y = y_hi * 2 + y_lo), z: 4, core: 2. Of those that a mesh axis runs over, the one named last changes fastest.
Arguments:
- wavefunction: bfloat16 [4, 1024, 1024], P('sector', 'ops'), may hold values from -6 to 6
- diag_scale: float32 [4, 1024, 1024], P('sector', 'ops'), may hold values from 1 to 8
- sector_dims: int32 [4], P('sector'), may hold values from 512 to 1024
- left_ops: bfloat16 [4, 64, 1024, 1024], P('sector', 'ops'), may hold values from -0.1875 to 0.1875
- right_ops: bfloat16 [4, 64, 1024, 1024], P('sector', 'ops'), may hold values from -0.1875 to 0.1875
- weight_index: int32 [4, 64], P('sector', 'ops'), may hold values from 0 to 15
- weight_table: float32 [16], replicated, may hold values from -1 to 1
Outputs:
- basis: bfloat16 [4, 1024, 1024], P('sector', 'ops')
- energy: float32 [4], P('sector')
- next_ops: float32 [1024, 1024], P('ops')
The draws below stay inside these ranges and needn't reach their ends.
All inputs are finite; a program needn't handle non-finite values.
Results may differ from the reference program's by a relative error of at most 0.025.
Values may be sent and summed in bfloat16 or wider, within the bound.
No kernel may reach another device: no remote copies, remote signals or barrier semaphores. Data moves between devices by JAX's collectives and lax.ppermute only.
A program may use at most 128 MiB of HBM per device.

```python
import math
import jax
import jax.numpy as jnp
from jax import lax

K = 1024
KEEP = 1024
NW = 16
GROUPS = 4
PAIRS = 64


def set_ends(entries, stream_key, smallest, largest):
    spot = [jax.random.randint(jax.random.fold_in(stream_key, axis), (), 0, length) for axis, length in enumerate(entries.shape)]
    main_axis = entries.shape.index(max(entries.shape))
    neighbour = spot[:main_axis] + [(spot[main_axis] + 1) % entries.shape[main_axis]] + spot[main_axis + 1:]
    return entries.at[tuple(spot)].set(smallest).at[tuple(neighbour)].set(largest)


def block_levels(own_key, shape, shards, low, high):
    level = 1.0
    for axis_at, parts in shards:
        heights = jax.random.uniform(jax.random.fold_in(jax.random.fold_in(own_key, 6), axis_at), (parts,), jnp.float32, low / len(shards), high / len(shards))
        level = level * jnp.repeat(jnp.exp(heights), shape[axis_at] // parts).reshape((-1,) + (1,) * (len(shape) - 1 - axis_at))
    return level


def bell_draw(stream_key, shape, deviation, most, pieces=(), held_as=jnp.bfloat16):
    values = deviation * jax.random.normal(stream_key, shape, jnp.float32)
    if pieces:
        values = values * block_levels(stream_key, shape, pieces, -0.22, 0.18)
    return jnp.clip(values, -most, most).astype(held_as)


def setup_inputs(seed: int = 0) -> dict:
    arg_keys = jax.random.split(jax.random.key(seed), 8)
    return {
        "wavefunction": bell_draw(arg_keys[0], (GROUPS, K, K), 1.0, 6.0, ((0, 4), (1, 32))),
        "diag_scale": jnp.clip(jnp.exp(math.log(8.0) - 2.0794415 * jax.random.uniform(arg_keys[1], (GROUPS, K, K), jnp.float32) ** block_levels(arg_keys[1], (GROUPS, K, K), ((0, 4), (1, 32)), -0.2, 0.2)), 1.0, 8.0),
        "sector_dims": set_ends(jax.random.randint(arg_keys[2], (GROUPS,), K // 2, K + 1), jax.random.fold_in(arg_keys[2], 1), K // 2, K).astype(jnp.int32),
        "left_ops": bell_draw(arg_keys[3], (GROUPS, PAIRS, K, K), K ** -0.5, 0.1875, ((0, 4), (1, 32))),
        "right_ops": bell_draw(arg_keys[4], (GROUPS, PAIRS, K, K), K ** -0.5, 0.1875, ((0, 4), (1, 32))),
        "weight_index": set_ends(jax.random.randint(arg_keys[5], (GROUPS, PAIRS), 0, NW), jax.random.fold_in(arg_keys[5], 1), 0, NW - 1).astype(jnp.int32),
        "weight_table": jnp.clip(jax.random.uniform(arg_keys[6], (NW,), jnp.float32, -1.0, 1.0), -1.0, 1.0),
    }


def group_step(psi, scale, dim, left, right, index, table):
    order_k = psi.shape[0]
    rows = jnp.arange(order_k)
    live = rows < dim
    mask = live[:, None] & live[None, :]
    psi_m = jnp.where(mask, psi, jnp.zeros_like(psi))
    onehot = (index[:, None] == jnp.arange(table.shape[0])[None, :]).astype(jnp.float32)
    coef = jnp.sum(onehot * table[None, :], axis=1)

    def add_pair(total, item):
        left_p, right_p, weight = item
        applied = jnp.dot(left_p.astype(jnp.float32), psi_m.astype(jnp.float32), preferred_element_type=jnp.float32).astype(jnp.bfloat16)
        term = lax.dot_general(applied.astype(jnp.float32), right_p.astype(jnp.float32), (((1,), (1,)), ((), ())), preferred_element_type=jnp.float32)
        return (total + weight * term, None)
    sigma, _ = lax.scan(add_pair, jnp.zeros((order_k, order_k), jnp.float32), (left, right, coef))
    sigma = jnp.where(mask, sigma, jnp.float32(0.0))
    psi_f = psi_m.astype(jnp.float32)
    energy = jnp.sum(psi_f * sigma) / jnp.sum(psi_f * psi_f)
    update = psi_f + (sigma - energy * psi_f) / scale
    columns = update[:, :KEEP]
    gram = jnp.dot(columns.T, columns, precision=lax.Precision.HIGHEST) / order_k
    gram = gram + 0.001 * jnp.eye(KEEP, dtype=jnp.float32)
    factor = jnp.linalg.cholesky(gram)
    basis = jax.scipy.linalg.solve_triangular(factor, columns.T, lower=True).T.astype(jnp.bfloat16)

    def rotate_pair(total, item):
        left_p, weight = item
        moved = jnp.dot(left_p.astype(jnp.float32), basis.astype(jnp.float32), preferred_element_type=jnp.float32).astype(jnp.bfloat16)
        rotated = jnp.dot(basis.T.astype(jnp.float32), moved.astype(jnp.float32), preferred_element_type=jnp.float32) / order_k
        return (total + weight * rotated, None)
    summed, _ = lax.scan(rotate_pair, jnp.zeros((KEEP, KEEP), jnp.float32), (left, coef))
    return (basis, energy, summed)

def reference(wavefunction, diag_scale, sector_dims, left_ops, right_ops, weight_index, weight_table):

    def one_group(items):
        psi, scale, dim, left, right, index = items
        return group_step(psi, scale, dim, left, right, index, weight_table)
    basis, energy, summed = lax.map(one_group, (wavefunction, diag_scale, sector_dims, left_ops, right_ops, weight_index))
    return (basis, energy, jnp.sum(summed, axis=0))
```

```python
import jax
import jax.numpy as jnp
from jax import lax
from jax.sharding import Mesh
from jax.sharding import PartitionSpec as P

OPS = ("ops_0", "ops_1", "ops_2")


def from_everyone(x, axis):
    count = lax.axis_size(axis)
    return lax.all_to_all(jnp.broadcast_to(x[None], (count, *x.shape)), axis, 0, 0, tiled=True)


def shards(wavefunction, diag_scale, sector_dims, left_ops, right_ops, weight_index, weight_table):
    psi_local = wavefunction[0]
    rows_dev, order_k = psi_local.shape
    owners = lax.axis_size(OPS)
    me = lax.axis_index(OPS)
    dim = sector_dims[0]
    live = jnp.arange(order_k) < dim
    row_live = me * rows_dev + jnp.arange(rows_dev) < dim
    psi_masked = jnp.where(row_live[:, None] & live[None, :], psi_local, jnp.bfloat16(0))
    psi = from_everyone(psi_masked, OPS).reshape(order_k, order_k)
    onehot = weight_index[0][:, None] == jnp.arange(weight_table.shape[0])[None, :]
    coef = jnp.sum(jnp.where(onehot, weight_table[None, :], jnp.float32(0)), axis=1)
    total = jnp.zeros((order_k, order_k), jnp.float32)
    for p in range(left_ops.shape[1]):
        applied = jnp.dot(left_ops[0, p], psi, preferred_element_type=jnp.float32)
        term = lax.dot_general(
            applied.astype(jnp.bfloat16),
            right_ops[0, p],
            (((1,), (1,)), ((), ())),
            preferred_element_type=jnp.float32,
        )
        total = total + coef[p] * term
    total = jnp.where(live[:, None] & live[None, :], total, jnp.float32(0))
    psi_f = psi.astype(jnp.float32)
    numer_part = jnp.sum(psi_f * total)
    denom = jnp.sum(psi_f * psi_f)
    arrived = lax.all_to_all(
        total.astype(jnp.bfloat16).reshape(owners, rows_dev, order_k), OPS, 0, 0, tiled=True
    )
    numer = jnp.sum(from_everyone(numer_part.reshape(1, 1), OPS))
    sigma = jnp.sum(arrived.astype(jnp.float32), axis=0)
    energy = numer / denom
    mine = psi_masked.astype(jnp.float32)
    update = mine + (sigma - energy * mine) / diag_scale[0]
    x = from_everyone(update.astype(jnp.bfloat16), OPS).reshape(order_k, order_k)
    gram = lax.dot_general(x, x, (((0,), (0,)), ((), ())), preferred_element_type=jnp.float32)
    gram = gram / order_k + 0.001 * jnp.eye(order_k, dtype=jnp.float32)
    factor = jnp.linalg.cholesky(gram)
    basis = jax.scipy.linalg.solve_triangular(factor, x.astype(jnp.float32).T, lower=True).T
    basis = basis.astype(jnp.bfloat16)
    mixed = coef[0] * left_ops[0, 0].astype(jnp.float32)
    for p in range(1, left_ops.shape[1]):
        mixed = mixed + coef[p] * left_ops[0, p].astype(jnp.float32)
    moved = jnp.dot(mixed.astype(jnp.bfloat16), basis, preferred_element_type=jnp.float32)
    summed = lax.dot_general(
        basis,
        moved.astype(jnp.bfloat16),
        (((0,), (0,)), ((), ())),
        preferred_element_type=jnp.float32,
    )
    summed = (summed / order_k).astype(jnp.bfloat16).reshape(owners, rows_dev, order_k)
    owned = jnp.sum(
        lax.all_to_all(summed, OPS, 0, 0, tiled=True).astype(jnp.float32), axis=0
    )
    next_rows = jnp.sum(
        from_everyone(owned.astype(jnp.bfloat16), "sector").astype(jnp.float32), axis=0
    )
    basis_local = lax.dynamic_slice_in_dim(basis, me * rows_dev, rows_dev, axis=0)
    return (basis_local[None], jnp.reshape(energy, (1,)), next_rows)


def solution(mesh):
    split = Mesh(
        mesh.devices.reshape(mesh.shape["sector"], 4, 4, 2), ("sector", "ops_0", "ops_1", "ops_2")
    )
    in_specs = (
        P("sector", OPS, None),
        P("sector", OPS, None),
        P("sector"),
        P("sector", OPS, None, None),
        P("sector", OPS, None, None),
        P("sector", OPS),
        P(),
    )
    out_specs = (P("sector", OPS, None), P("sector"), P(OPS, None))
    return jax.shard_map(
        shards, mesh=split, in_specs=in_specs, out_specs=out_specs, check_vma=False
    )
```

```python
import jax
import jax.numpy as jnp
from jax import lax
from jax.experimental import pallas as pl
from jax.experimental.pallas import tpu as pltpu
from jax.sharding import Mesh
from jax.sharding import PartitionSpec as P

OPS = ("ops_0", "ops_1", "ops_2")
F32, BF16 = jnp.float32, jnp.bfloat16
NB = 128


def two(x):
    hi = x.astype(BF16)
    return hi, (x - hi.astype(F32)).astype(BF16)


def three(x):
    hi = x.astype(BF16)
    rest = x - hi.astype(F32)
    mid = rest.astype(BF16)
    return hi, mid, (rest - mid.astype(F32)).astype(BF16)


def mm(a, b, dims):
    return lax.dot_general(a, b, (dims, ((), ())), preferred_element_type=F32)


def mm6(a, b, dims):
    (ah, am, al), (bh, bm, bl) = a, b
    small = mm(al, bh, dims) + mm(ah, bl, dims) + mm(am, bm, dims)
    return small + (mm(am, bh, dims) + mm(ah, bm, dims)) + mm(ah, bh, dims)


def mm3(a, b, dims):
    (ah, al), (bh, bl) = a, b
    return mm(al, bh, dims) + mm(ah, bl, dims) + mm(ah, bh, dims)


def wide(x):
    return jnp.broadcast_to(x, (8, NB))


def stacked(rows):
    at = lax.broadcasted_iota(jnp.int32, (8, NB), 0)
    out = rows[0]
    for i in range(1, 8):
        out = jnp.where(at == i, rows[i], out)
    return out


def inverse_factor(block):
    panels = NB // 8
    a = [block[8 * i : 8 * i + 8] for i in range(panels)]
    row = lax.broadcasted_iota(jnp.int32, (NB, NB), 0)
    col = lax.broadcasted_iota(jnp.int32, (NB, NB), 1)
    eye = jnp.where(row == col, F32(1), F32(0))
    e = [eye[8 * i : 8 * i + 8] for i in range(panels)]
    done = []
    for p in range(panels):
        cols = [wide(a[p][:, 8 * p + j : 8 * p + j + 1]) for j in range(8)]
        s = {(i, j): wide(cols[j][i : i + 1]) for j in range(8) for i in range(j, 8)}
        u = [wide(a[p][i : i + 1]) for i in range(8)]
        w = [wide(e[p][i : i + 1]) for i in range(8)]
        last = p == panels - 1
        v = None if last else [wide(a[p + 1][:, 8 * p + j : 8 * p + j + 1]) for j in range(8)]
        nxt = None if last else a[p + 1]
        us, ws = [], []
        for k in range(8):
            d = s[k, k]
            r = pl.reciprocal(d, approx=True)
            r = r * (2.0 - d * r)
            q = lax.rsqrt(d)
            q = q * (1.5 - 0.5 * d * (q * q))
            f = {i: s[i, k] * r for i in range(k + 1, 8)}
            for i in range(k + 1, 8):
                for j in range(k + 1, i + 1):
                    s[i, j] = s[i, j] - f[i] * s[j, k]
                u[i] = u[i] - f[i] * u[k]
                w[i] = w[i] - f[i] * w[k]
                if not last:
                    v[i] = v[i] - f[i] * v[k]
            if not last:
                nxt = nxt - (v[k] * r) * u[k]
                us.append(u[k] * q)
            ws.append(w[k] * q)
        wp = stacked(ws)
        done.append(wp)
        if last:
            break
        up = stacked(us)
        a[p + 1] = nxt
        both = jnp.concatenate([up, wp], axis=1)
        h = both.astype(BF16).astype(F32)
        m = (both - h).astype(BF16).astype(F32)
        t = both - h - m
        left = jnp.concatenate([x[:, :NB] for x in (h, h, m, m, h, t)], axis=0).astype(BF16)
        right = jnp.concatenate([h, m, h, m, t, h], axis=0).astype(BF16)
        out = mm(left, right, ((0,), (0,)))
        for i in range(p + 1, panels):
            if i > p + 1:
                a[i] = a[i] - out[8 * i : 8 * i + 8, :NB]
            e[i] = e[i] - out[8 * i : 8 * i + 8, NB:]
    return jnp.concatenate(done, axis=0)


def basis_kernel(x_ref, g_ref, b_ref, bl_ref, uh_ref, um_ref, ul_ref, pan_ref):
    n = x_ref.shape[0]
    for ref in (b_ref, bl_ref, uh_ref, um_ref, ul_ref):
        ref[...] = jnp.zeros_like(ref)

    def step(k, carry):
        at = pl.ds(pl.multiple_of(k * NB, NB), NB)
        mine = tuple(ref[:, at] for ref in (uh_ref, um_ref, ul_ref))
        whole = tuple(ref[...] for ref in (uh_ref, um_ref, ul_ref))
        pan_ref[...] = g_ref[at, :] - mm6(mine, whole, ((0,), (0,)))
        w = inverse_factor(pan_ref[:, at])
        u = mm6(three(w), three(pan_ref[...]), ((1,), (0,)))
        for ref, part in zip((uh_ref, um_ref, ul_ref), three(u)):
            ref[at, :] = part
        rest = x_ref[:, at].astype(F32) - mm3(
            (b_ref[...], bl_ref[...]), (uh_ref[:, at], um_ref[:, at]), ((1,), (0,))
        )
        new = mm3(two(rest), two(w), ((1,), (1,)))
        hi, lo = two(new)
        b_ref[:, at] = hi
        bl_ref[:, at] = lo
        return carry

    lax.fori_loop(0, n // NB, step, 0)


def basis_of(x, gram):
    n = x.shape[0]
    square = lambda t: pltpu.VMEM((n, n), t)
    return pl.pallas_call(
        basis_kernel,
        out_shape=jax.ShapeDtypeStruct((n, n), BF16),
        in_specs=[pl.BlockSpec(memory_space=pltpu.VMEM)] * 2,
        out_specs=pl.BlockSpec(memory_space=pltpu.VMEM),
        scratch_shapes=[square(BF16)] * 4 + [pltpu.VMEM((NB, n), F32)],
        compiler_params=pltpu.CompilerParams(vmem_limit_bytes=56 * 2**20),
    )(x, gram)


def from_everyone(x, axis):
    count = lax.axis_size(axis)
    return lax.all_to_all(jnp.broadcast_to(x[None], (count, *x.shape)), axis, 0, 0, tiled=True)


def shards(wavefunction, diag_scale, sector_dims, left_ops, right_ops, weight_index, weight_table):
    psi_local = wavefunction[0]
    rows_dev, order_k = psi_local.shape
    owners = lax.axis_size(OPS)
    me = lax.axis_index(OPS)
    dim = sector_dims[0]
    live = jnp.arange(order_k) < dim
    row_live = me * rows_dev + jnp.arange(rows_dev) < dim
    psi_masked = jnp.where(row_live[:, None] & live[None, :], psi_local, jnp.bfloat16(0))
    psi = from_everyone(psi_masked, OPS).reshape(order_k, order_k)
    onehot = weight_index[0][:, None] == jnp.arange(weight_table.shape[0])[None, :]
    coef = jnp.sum(jnp.where(onehot, weight_table[None, :], jnp.float32(0)), axis=1)
    total = jnp.zeros((order_k, order_k), jnp.float32)
    for p in range(left_ops.shape[1]):
        applied = jnp.dot(left_ops[0, p], psi, preferred_element_type=jnp.float32)
        term = lax.dot_general(
            applied.astype(jnp.bfloat16),
            right_ops[0, p],
            (((1,), (1,)), ((), ())),
            preferred_element_type=jnp.float32,
        )
        total = total + coef[p] * term
    total = jnp.where(live[:, None] & live[None, :], total, jnp.float32(0))
    psi_f = psi.astype(jnp.float32)
    numer_part = jnp.sum(psi_f * total)
    denom = jnp.sum(psi_f * psi_f)
    high, mid, low = three(numer_part)
    lane = jnp.arange(NB)
    tail = jnp.where(lane == 0, high, jnp.where(lane == 1, mid, jnp.where(lane == 2, low, 0)))
    tail = jnp.broadcast_to(tail.astype(BF16), (order_k, NB))
    sent = jnp.concatenate([total.astype(BF16), tail], axis=1)
    arrived = lax.all_to_all(
        sent.reshape(owners, rows_dev, order_k + NB), OPS, 0, 0, tiled=True
    ).astype(F32)
    sigma = jnp.sum(arrived[:, :, :order_k], axis=0)
    numer = jnp.sum(arrived[:, 0, order_k:])
    energy = numer / denom
    mine = psi_masked.astype(jnp.float32)
    update = mine + (sigma - energy * mine) / diag_scale[0]
    x = from_everyone(update.astype(jnp.bfloat16), OPS).reshape(order_k, order_k)
    gram = lax.dot_general(x, x, (((0,), (0,)), ((), ())), preferred_element_type=jnp.float32)
    gram = gram / order_k + 0.001 * jnp.eye(order_k, dtype=jnp.float32)
    basis = basis_of(x, gram)
    mixed = coef[0] * left_ops[0, 0].astype(jnp.float32)
    for p in range(1, left_ops.shape[1]):
        mixed = mixed + coef[p] * left_ops[0, p].astype(jnp.float32)
    moved = jnp.dot(mixed.astype(jnp.bfloat16), basis, preferred_element_type=jnp.float32)
    summed = lax.dot_general(
        basis,
        moved.astype(jnp.bfloat16),
        (((0,), (0,)), ((), ())),
        preferred_element_type=jnp.float32,
    )
    summed = (summed / order_k).astype(jnp.bfloat16).reshape(owners, rows_dev, order_k)
    owned = jnp.sum(
        lax.all_to_all(summed, OPS, 0, 0, tiled=True).astype(jnp.float32), axis=0
    )
    owned = owned.astype(BF16)
    groups = lax.axis_size("sector")
    near, far, cross = (
        lax.ppermute(owned, "sector", [(i, i ^ d) for i in range(groups)]).astype(F32)
        for d in (1, 2, 3)
    )
    next_rows = (owned.astype(F32) + near) + (far + cross)
    basis_local = lax.dynamic_slice_in_dim(basis, me * rows_dev, rows_dev, axis=0)
    return (basis_local[None], jnp.reshape(energy, (1,)), next_rows)


def solution(mesh):
    split = Mesh(
        mesh.devices.reshape(mesh.shape["sector"], 4, 4, 2), ("sector", "ops_0", "ops_1", "ops_2")
    )
    in_specs = (
        P("sector", OPS, None),
        P("sector", OPS, None),
        P("sector"),
        P("sector", OPS, None, None),
        P("sector", OPS, None, None),
        P("sector", OPS),
        P(),
    )
    out_specs = (P("sector", OPS, None), P("sector"), P(OPS, None))
    return jax.shard_map(
        shards, mesh=split, in_specs=in_specs, out_specs=out_specs, check_vma=False
    )
```

```python
import jax
import jax.numpy as jnp
from jax import lax
from jax.experimental import pallas as pl
from jax.experimental.pallas import tpu as pltpu
from jax.sharding import Mesh
from jax.sharding import PartitionSpec as P

OPS = ("ops_0", "ops_1", "ops_2")
F32, BF16 = jnp.float32, jnp.bfloat16
NB = 128


def two(x):
    hi = x.astype(BF16)
    return hi, (x - hi.astype(F32)).astype(BF16)


def three(x):
    hi = x.astype(BF16)
    rest = x - hi.astype(F32)
    mid = rest.astype(BF16)
    return hi, mid, (rest - mid.astype(F32)).astype(BF16)


def mm(a, b, dims):
    return lax.dot_general(a, b, (dims, ((), ())), preferred_element_type=F32)


def mm6(a, b, dims):
    (ah, am, al), (bh, bm, bl) = a, b
    small = mm(al, bh, dims) + mm(ah, bl, dims) + mm(am, bm, dims)
    return small + (mm(am, bh, dims) + mm(ah, bm, dims)) + mm(ah, bh, dims)


def mm3(a, b, dims):
    (ah, al), (bh, bl) = a, b
    return mm(al, bh, dims) + mm(ah, bl, dims) + mm(ah, bh, dims)


def wide(x):
    return jnp.broadcast_to(x, (8, NB))


def stacked(rows):
    at = lax.broadcasted_iota(jnp.int32, (8, NB), 0)
    out = rows[0]
    for i in range(1, 8):
        out = jnp.where(at == i, rows[i], out)
    return out


def inv_sqrt(d):
    q = lax.rsqrt(d)
    return q * (1.5 - 0.5 * d * (q * q))


def inverse_factor(block):
    panels = NB // 8
    a = [block[8 * i : 8 * i + 8] for i in range(panels)]
    row = lax.broadcasted_iota(jnp.int32, (NB, NB), 0)
    col = lax.broadcasted_iota(jnp.int32, (NB, NB), 1)
    eye = jnp.where(row == col, F32(1), F32(0))
    e = [eye[8 * i : 8 * i + 8] for i in range(panels)]
    done = []
    for p in range(panels):
        cols = [wide(a[p][:, 8 * p + j : 8 * p + j + 1]) for j in range(8)]
        s = {(i, j): wide(cols[j][i : i + 1]) for j in range(8) for i in range(j, 8)}
        u = [wide(a[p][i : i + 1]) for i in range(8)]
        w = [wide(e[p][i : i + 1]) for i in range(8)]
        last = p == panels - 1
        v = None if last else [wide(a[p + 1][:, 8 * p + j : 8 * p + j + 1]) for j in range(8)]
        nxt = None if last else a[p + 1]
        us, ws = [], []
        for k in range(0, 8, 2):
            d0, c, d1 = s[k, k], s[k + 1, k], s[k + 1, k + 1]
            det = d0 * d1 - c * c
            rd = pl.reciprocal(det, approx=True)
            rd = rd * (2.0 - det * rd)
            r0 = pl.reciprocal(d0, approx=True)
            r0 = r0 * (2.0 - d0 * r0)
            q0, q1 = inv_sqrt(d0), inv_sqrt(det * r0)
            f0, f1 = {}, {}
            for i in range(k + 2, 8):
                f0[i] = (s[i, k] * d1 - s[i, k + 1] * c) * rd
                f1[i] = (s[i, k + 1] * d0 - s[i, k] * c) * rd
            for i in range(k + 2, 8):
                for j in range(k + 2, i + 1):
                    s[i, j] = s[i, j] - (f0[i] * s[j, k] + f1[i] * s[j, k + 1])
            g = c * r0

            def swept(rows):
                for i in range(k + 2, 8):
                    rows[i] = rows[i] - (f0[i] * rows[k] + f1[i] * rows[k + 1])
                return rows[k] * q0, (rows[k + 1] - g * rows[k]) * q1

            ws.extend(swept(w))
            if not last:
                u0, u1 = swept(u)
                v0, v1 = swept(v)
                nxt = nxt - (v0 * u0 + v1 * u1)
                us.extend((u0, u1))
        wp = stacked(ws)
        done.append(wp)
        if last:
            break
        up = stacked(us)
        a[p + 1] = nxt
        both = jnp.concatenate([up, wp], axis=1)
        h = both.astype(BF16).astype(F32)
        m = (both - h).astype(BF16).astype(F32)
        t = both - h - m
        left = jnp.concatenate([x[:, :NB] for x in (h, h, m, m, h, t)], axis=0).astype(BF16)
        right = jnp.concatenate([h, m, h, m, t, h], axis=0).astype(BF16)
        out = mm(left, right, ((0,), (0,)))
        for i in range(p + 1, panels):
            if i > p + 1:
                a[i] = a[i] - out[8 * i : 8 * i + 8, :NB]
            e[i] = e[i] - out[8 * i : 8 * i + 8, NB:]
    return jnp.concatenate(done, axis=0)


def factor_half(g_ref, x_ref, bh_ref, bm_ref, u_refs, w_ref, pan_ref, ready=None):
    half = g_ref.shape[0]

    def parts(rows, cols):
        return tuple(ref[rows, cols] for ref in u_refs)

    def step(k, carry):
        for j in range(half // NB):
            lo = NB * j

            @pl.when(k == j)
            def _():
                acc = g_ref[lo : lo + NB, lo:]
                if j:
                    above = slice(0, lo)
                    acc = acc - mm6(
                        parts(above, slice(lo, lo + NB)), parts(above, slice(lo, half)), ((0,), (0,))
                    )
                pan_ref[:, : half - lo] = acc

        w_ref[pl.ds(pl.multiple_of(k * NB, NB), NB), :] = inverse_factor(pan_ref[:, :NB])
        for j in range(half // NB):
            lo = NB * j

            @pl.when(k == j)
            def _():
                w = w_ref[lo : lo + NB, :]
                u = mm6(three(w), three(pan_ref[:, : half - lo]), ((1,), (0,)))
                for ref, part in zip(u_refs, three(u)):
                    ref[lo : lo + NB, lo:] = part
                if ready is not None:
                    ready(j, False)
                if j % 2:
                    c, hi = lo - NB, lo + NB
                    above, pair = slice(0, c), slice(c, hi)
                    rest = x_ref[:, pair].astype(F32)
                    if c:
                        rest = rest - mm3(
                            (bh_ref[:, above], bm_ref[:, above]), parts(above, pair)[:2], ((1,), (0,))
                        )
                    first = w_ref[c:lo, :]
                    cross = mm6(parts(slice(c, lo), slice(lo, hi)), three(first), ((0,), (0,)))
                    cross = mm6(three(w), three(cross), ((1,), (0,)))
                    both = jnp.concatenate(
                        [
                            jnp.concatenate([first, jnp.zeros_like(first)], axis=1),
                            jnp.concatenate([-cross, w], axis=1),
                        ],
                        axis=0,
                    )
                    new = mm3(two(rest), two(both), ((1,), (1,)))
                    bh_ref[:, pair], bm_ref[:, pair] = two(new)
                    if ready is not None:
                        ready(j, True)

        return carry

    lax.fori_loop(0, half // NB, step, 0)


def gram_of(x, n):
    half = x.shape[1]
    row = lax.broadcasted_iota(jnp.int32, (half, half), 0)
    col = lax.broadcasted_iota(jnp.int32, (half, half), 1)
    return mm(x, x, ((0,), (0,))) * (1.0 / n) + jnp.where(row == col, F32(0.001), F32(0))


def first_kernel(x_ref, *refs):
    out, held, (g_ref, pan_ref, sems) = refs[:6], refs[6:12], refs[12:]
    bh_ref, bm_ref, uh_ref, um_ref, ul_ref, w_ref = held
    half = x_ref.shape[1]

    def pieces(j, basis):
        rows = slice(NB * j, NB * (j + 1))
        pair = slice(NB * (j - 1), NB * (j + 1))
        if basis:
            which = [(i, (slice(None), pair)) for i in (0, 1)]
        else:
            which = [(i, (rows, slice(NB * j, half))) for i in (2, 3, 4)] + [(5, (rows, slice(None)))]
        return [pltpu.make_async_copy(held[i].at[at], out[i].at[at], sems.at[i, j]) for i, at in which]

    def send(j, basis):
        for copy in pieces(j, basis):
            copy.start()

    g_ref[...] = gram_of(x_ref[...], x_ref.shape[0])
    factor_half(g_ref, x_ref, bh_ref, bm_ref, (uh_ref, um_ref, ul_ref), w_ref, pan_ref, send)
    for j in range(half // NB):
        for copy in pieces(j, False) + (pieces(j, True) if j % 2 else []):
            copy.wait()


def second_kernel(place_ref, *refs):
    given, (rows_ref, give_ref, keep_ref), held, rest = refs[:9], refs[9:12], refs[12:20], refs[20:]
    basis_ref, bm_ref, uh_ref, um_ref, ul_ref, vh_ref, vm_ref, vl_ref = rest[:8]
    w_ref, g_ref, x_ref, pan_ref, moved_ref, sems = rest[8:]
    x2_ref, x1_ref, w1_ref, u1h_ref, u1m_ref, u1l_ref, b1m_ref, mixed_ref = held
    n, half = x2_ref.shape
    left, right = (basis_ref.at[:, slice(c, c + half)] for c in (0, half))
    copies = [
        pltpu.make_async_copy(a, b, sems.at[i]) for i, (a, b) in enumerate(zip(given, (*held[:7], left, held[7])))
    ]
    for copy in copies:
        copy.start()
    u1 = (u1h_ref, u1m_ref, u1l_ref)
    cross = (vh_ref, vm_ref, vl_ref)
    copies[0].wait()
    x2 = x2_ref[...]
    g_ref[...] = gram_of(x2, n)
    for copy in copies[1:6]:
        copy.wait()
    for j in range(half // NB):
        lo = NB * j
        mine = slice(lo, lo + NB)
        acc = mm(x1_ref[:, mine], x2, ((0,), (0,))) * (1.0 / n)
        if j:
            acc = acc - mm6(
                tuple(ref[:lo, mine] for ref in u1), tuple(ref[:lo, :] for ref in cross), ((0,), (0,))
            )
        for ref, part in zip(cross, three(mm6(three(w1_ref[mine, :]), three(acc), ((1,), (0,))))):
            ref[mine, :] = part
    whole = tuple(ref[...] for ref in cross)
    g_ref[...] = g_ref[...] - mm6(whole, whole, ((0,), (0,)))
    for copy in copies[6:8]:
        copy.wait()
    x_ref[...] = x2.astype(F32) - mm3((basis_ref[:, :half], b1m_ref[...]), whole[:2], ((1,), (0,)))
    factor_half(g_ref, x_ref, right, bm_ref, (uh_ref, um_ref, ul_ref), w_ref, pan_ref)
    me, core = place_ref[0], place_ref[1]
    own = rows_ref.shape[0]
    rows_ref[...] = basis_ref[pl.ds(pl.multiple_of(me * own, own), own), :]
    copies[8].wait()
    moved_ref[...] = mm(mixed_ref[...], basis_ref[...], ((1,), (0,))).astype(BF16)
    for ref, side in ((give_ref, 1 - core), (keep_ref, core)):
        cols = moved_ref[:, pl.ds(pl.multiple_of(side * half, half), half)]
        ref[...] = (mm(basis_ref[...], cols, ((0,), (0,))) * (1.0 / n)).astype(BF16)


VMEM = pl.BlockSpec(memory_space=pltpu.VMEM)
SMEM = pl.BlockSpec(memory_space=pltpu.SMEM)
HBM = pl.BlockSpec(memory_space=pltpu.HBM)


def basis_and_rotation(x1, x2, mixed, place, own):
    n, half = x1.shape
    sds = jax.ShapeDtypeStruct
    tall, square = sds((n, half), BF16), sds((half, half), BF16)
    strip = sds((half, NB), F32)
    params = pltpu.CompilerParams(vmem_limit_bytes=60 * 2**20)
    g, pan = pltpu.VMEM((half, half), F32), pltpu.VMEM((NB, half), F32)
    out = [tall, tall, square, square, square, strip]
    bh, bm, uh, um, ul, w = pl.pallas_call(
        first_kernel,
        out_shape=out,
        in_specs=[VMEM],
        out_specs=[HBM] * len(out),
        scratch_shapes=[pltpu.VMEM(a.shape, a.dtype) for a in out]
        + [g, pan, pltpu.SemaphoreType.DMA((len(out), half // NB))],
        compiler_params=params,
    )(x1)
    operands = (x2, x1, w, uh, um, ul, bm, bh, mixed)
    waiting = operands[:7] + operands[8:]
    quarter = sds((n, half), BF16)
    return pl.pallas_call(
        second_kernel,
        out_shape=[sds((own, n), BF16), quarter, quarter],
        in_specs=[SMEM] + [HBM] * len(operands),
        out_specs=[VMEM] * 3,
        scratch_shapes=[pltpu.VMEM(a.shape, a.dtype) for a in waiting]
        + [pltpu.VMEM((n, n), BF16), pltpu.VMEM((n, half), BF16)]
        + [pltpu.VMEM((half, half), BF16)] * 6
        + [pltpu.VMEM((half, NB), F32), g, pltpu.VMEM((n, half), F32), pan]
        + [pltpu.VMEM((n, n), BF16), pltpu.SemaphoreType.DMA((len(operands),))],
        compiler_params=params,
    )(place, *operands)


def sigma_kernel(
    coef_ref, dim_ref, psi_ref, left_hbm, right_hbm, sent_ref, denom_ref, mixed_hbm,
    app_ref, left_ref, right_ref, mixed_ref, sems,
):
    n = psi_ref.shape[0]
    step = 256
    count = left_ref.shape[0]
    pairs = range(count)
    dim = dim_ref[0]
    blocks = [(p, slice(r, r + n // 2)) for p in pairs for r in (0, n // 2)]

    def fetch(source, held, at):
        return [
            pltpu.make_async_copy(source.at[0, p, rows, :], held.at[p, rows, :], sems.at[at, i])
            for i, (p, rows) in enumerate(blocks)
        ]

    lefts, rights = fetch(left_hbm, left_ref, 0), fetch(right_hbm, right_ref, 1)
    for copy in lefts + rights:
        copy.start()
    for copy, (p, rows) in zip(lefts, blocks):
        copy.wait()
        app_ref[p, rows, :] = mm(left_ref[p, rows, :], psi_ref[...], ((1,), (0,))).astype(BF16)
    for copy in rights:
        copy.wait()
    mixed = coef_ref[0] * left_ref[0].astype(F32)
    for p in pairs[1:]:
        mixed = mixed + coef_ref[p] * left_ref[p].astype(F32)
    mixed_ref[...] = mixed.astype(BF16)
    put = pltpu.make_async_copy(mixed_ref, mixed_hbm, sems.at[2, 0])
    put.start()
    row = lax.broadcasted_iota(jnp.int32, (n, step), 0)
    numer, denom = F32(0), F32(0)
    for c in range(0, n, step):
        cols = slice(c, c + step)
        total = jnp.zeros((n, step), F32)
        for p in pairs:
            total = total + coef_ref[p] * mm(app_ref[p], right_ref[p, cols, :], ((1,), (1,)))
        col = lax.broadcasted_iota(jnp.int32, (n, step), 1) + c
        total = jnp.where((row < dim) & (col < dim), total, F32(0))
        psi = psi_ref[:, cols].astype(F32)
        numer = numer + jnp.sum(psi * total)
        denom = denom + jnp.sum(psi * psi)
        sent_ref[:, cols] = total.astype(BF16)
    lane = lax.broadcasted_iota(jnp.int32, (n, NB), 1)
    numer = jnp.full((n, NB), numer, F32)
    high, mid, low = (part.astype(F32) for part in three(numer))
    tail = jnp.where(lane == 0, high, jnp.where(lane == 1, mid, jnp.where(lane == 2, low, F32(0))))
    sent_ref[:, n:] = tail.astype(BF16)
    denom_ref[0] = denom
    put.wait()


def sigma_part(coef, dim, psi, left_ops, right_ops):
    n = psi.shape[0]
    sds = jax.ShapeDtypeStruct
    return pl.pallas_call(
        sigma_kernel,
        out_shape=[sds((n, n + NB), BF16), sds((1,), F32), sds((n, n), BF16)],
        in_specs=[SMEM, SMEM, VMEM, HBM, HBM],
        out_specs=[VMEM, SMEM, HBM],
        scratch_shapes=[pltpu.VMEM(left_ops.shape[1:], BF16)] * 3
        + [pltpu.VMEM((n, n), BF16), pltpu.SemaphoreType.DMA((3, 2 * left_ops.shape[1]))],
        compiler_params=pltpu.CompilerParams(vmem_limit_bytes=58 * 2**20),
    )(coef, dim, psi, left_ops, right_ops)


def from_everyone(x, axis):
    count = lax.axis_size(axis)
    return lax.all_to_all(jnp.broadcast_to(x[None], (count, *x.shape)), axis, 0, 0, tiled=True)


def rows_of_all(x):
    got = from_everyone(x, OPS)
    return got.reshape(-1, got.shape[-1])


def to_owners(x):
    tiles = x.reshape(lax.axis_size(OPS), -1, x.shape[-1])
    return lax.all_to_all(tiles, OPS, 0, 0, tiled=True).astype(F32)


def shards(wavefunction, diag_scale, sector_dims, left_ops, right_ops, weight_index, weight_table):
    psi_local = wavefunction[0]
    rows_dev, order_k = psi_local.shape
    half = order_k // 2
    me = lax.axis_index(OPS)
    dim = sector_dims[0]
    live = jnp.arange(order_k) < dim
    row_live = me * rows_dev + jnp.arange(rows_dev) < dim
    mine = jnp.where(row_live[:, None] & live[None, :], psi_local, BF16(0))
    psi = rows_of_all(mine)
    onehot = weight_index[0][:, None] == jnp.arange(weight_table.shape[0])[None, :]
    coef = jnp.sum(jnp.where(onehot, weight_table[None, :], F32(0)), axis=1)
    sent, denom, mixed = sigma_part(coef, sector_dims, psi, left_ops, right_ops)
    arrived = to_owners(sent)
    sigma = jnp.sum(arrived[:, :, :order_k], axis=0)
    energy = jnp.sum(arrived[:, 0, order_k:]) / denom[0]
    old = mine.astype(F32)
    update = (old + (sigma - energy * old) / diag_scale[0]).astype(BF16)
    x = [rows_of_all(update[:, h]) for h in (slice(0, half), slice(half, order_k))]
    core = lax.axis_index("sector") % 2
    place = jnp.stack([me, core]).astype(jnp.int32)
    basis_local, give, keep = basis_and_rotation(*x, mixed, place, rows_dev)

    def swapped(values, bits):
        count = lax.axis_size("sector")
        return lax.ppermute(values, "sector", [(i, i ^ bits) for i in range(count)])

    kept = (keep.astype(F32) + swapped(give, 1).astype(F32)).astype(BF16)
    owned = jnp.sum(to_owners(kept), axis=0).astype(BF16)
    near, far, cross = (swapped(owned, bits).astype(F32) for bits in (1, 2, 3))
    own, other = owned.astype(F32) + far, near + cross
    next_rows = jnp.concatenate(
        [jnp.where(core == 0, own, other), jnp.where(core == 0, other, own)], axis=1
    )
    return (basis_local[None], jnp.reshape(energy, (1,)), next_rows)


def solution(mesh):
    split = Mesh(
        mesh.devices.reshape(mesh.shape["sector"], 4, 4, 2), ("sector", "ops_0", "ops_1", "ops_2")
    )
    in_specs = (
        P("sector", OPS, None),
        P("sector", OPS, None),
        P("sector"),
        P("sector", OPS, None, None),
        P("sector", OPS, None, None),
        P("sector", OPS),
        P(),
    )
    out_specs = (P("sector", OPS, None), P("sector"), P(OPS, None))
    return jax.shard_map(
        shards, mesh=split, in_specs=in_specs, out_specs=out_specs, check_vma=False
    )
```

```python
import jax
import jax.numpy as jnp
from jax import lax
from jax.experimental import pallas as pl
from jax.experimental.pallas import tpu as pltpu
from jax.sharding import Mesh
from jax.sharding import PartitionSpec as P

OPS = ("ops_0", "ops_1", "ops_2")
F32, BF16 = jnp.float32, jnp.bfloat16
NB = 128


def two(x):
    hi = x.astype(BF16)
    return hi, (x - hi.astype(F32)).astype(BF16)


def three(x):
    hi = x.astype(BF16)
    rest = x - hi.astype(F32)
    mid = rest.astype(BF16)
    return hi, mid, (rest - mid.astype(F32)).astype(BF16)


def mm(a, b, dims):
    return lax.dot_general(a, b, (dims, ((), ())), preferred_element_type=F32)


def mm6(a, b, dims):
    (ah, am, al), (bh, bm, bl) = a, b
    small = mm(al, bh, dims) + mm(ah, bl, dims) + mm(am, bm, dims)
    return small + (mm(am, bh, dims) + mm(ah, bm, dims)) + mm(ah, bh, dims)


def mm3(a, b, dims):
    (ah, al), (bh, bl) = a, b
    return mm(al, bh, dims) + mm(ah, bl, dims) + mm(ah, bh, dims)


def wide(x):
    return jnp.broadcast_to(x, (8, NB))


def stacked(rows):
    at = lax.broadcasted_iota(jnp.int32, (8, NB), 0)
    out = rows[0]
    for i in range(1, 8):
        out = jnp.where(at == i, rows[i], out)
    return out


def inv_sqrt(d):
    q = lax.rsqrt(d)
    return q * (1.5 - 0.5 * d * (q * q))


def inverse_factor(block, tasks=()):
    tasks = list(tasks)
    slots = len(tasks)
    panels = NB // 8
    a = [block[8 * i : 8 * i + 8] for i in range(panels)]
    row = lax.broadcasted_iota(jnp.int32, (NB, NB), 0)
    col = lax.broadcasted_iota(jnp.int32, (NB, NB), 1)
    eye = jnp.where(row == col, F32(1), F32(0))
    e = [eye[8 * i : 8 * i + 8] for i in range(panels)]
    done = []
    for p in range(panels):
        cols = [wide(a[p][:, 8 * p + j : 8 * p + j + 1]) for j in range(8)]
        s = {(i, j): wide(cols[j][i : i + 1]) for j in range(8) for i in range(j, 8)}
        u = [wide(a[p][i : i + 1]) for i in range(8)]
        w = [wide(e[p][i : i + 1]) for i in range(8)]
        last = p == panels - 1
        v = None if last else [wide(a[p + 1][:, 8 * p + j : 8 * p + j + 1]) for j in range(8)]
        nxt = None if last else a[p + 1]
        us, ws = [], []
        for k in range(0, 8, 2):
            d0, c, d1 = s[k, k], s[k + 1, k], s[k + 1, k + 1]
            det = d0 * d1 - c * c
            rd = pl.reciprocal(det, approx=True)
            fix = 2.0 - det * rd
            n0 = {i: s[i, k] * d1 - s[i, k + 1] * c for i in range(k + 2, 8)}
            n1 = {i: s[i, k + 1] * d0 - s[i, k] * c for i in range(k + 2, 8)}
            soon = [(i, j) for j in range(k + 2, 4 + k) for i in range(j, 4 + k)] if k < 6 else []
            for i, j in soon:
                taken = n0[i] * s[j, k] + n1[i] * s[j, k + 1]
                s[i, j] = s[i, j] - (taken * rd) * fix
            rd = rd * fix
            f0 = {i: n0[i] * rd for i in n0}
            f1 = {i: n1[i] * rd for i in n1}
            for i in range(k + 2, 8):
                for j in range(k + 2, i + 1):
                    if (i, j) not in soon:
                        s[i, j] = s[i, j] - (f0[i] * s[j, k] + f1[i] * s[j, k + 1])
            r0 = pl.reciprocal(d0, approx=True)
            r0 = r0 * (2.0 - d0 * r0)
            q0, q1 = inv_sqrt(d0), inv_sqrt(det * r0)
            g = c * r0

            def swept(rows):
                for i in range(k + 2, 8):
                    rows[i] = rows[i] - (f0[i] * rows[k] + f1[i] * rows[k + 1])
                return rows[k] * q0, (rows[k + 1] - g * rows[k]) * q1

            ws.extend(swept(w))
            if not last:
                us.extend(swept(u))
                v0, v1 = v[k], v[k + 1]
                swept(v)
                both = ((v0 * d1 - v1 * c) * u[k] + (v1 * d0 - v0 * c) * u[k + 1]) * rd
                nxt = nxt - both
        while tasks and (slots - len(tasks)) * (panels - 3) < slots * p:
            tasks.pop(0)()
        wp = stacked(ws)
        done.append(wp)
        if last:
            break
        up = stacked(us)
        a[p + 1] = nxt
        both = jnp.concatenate([up, wp], axis=1)
        h = both.astype(BF16).astype(F32)
        m = (both - h).astype(BF16).astype(F32)
        t = both - h - m
        left = jnp.concatenate([x[:, :NB] for x in (h, h, m, m, h, t)], axis=0).astype(BF16)
        right = jnp.concatenate([h, m, h, m, t, h], axis=0).astype(BF16)
        out = mm(left, right, ((0,), (0,)))
        for i in range(p + 1, panels):
            if i > p + 1:
                a[i] = a[i] - out[8 * i : 8 * i + 8, :NB]
            e[i] = e[i] - out[8 * i : 8 * i + 8, NB:]
    return jnp.concatenate(done, axis=0)


def joined(a, b, a_dim, b_dim):
    (ah, am, al), (bh, bm, bl) = a, b
    left = jnp.concatenate([al, ah, am, am, ah, ah], axis=a_dim)
    right = jnp.concatenate([bh, bl, bm, bh, bm, bh], axis=b_dim)
    return mm(left, right, ((a_dim,), (b_dim,)))


def parts(refs, rows, cols):
    return tuple(ref[rows, cols] for ref in refs)


def put(refs, rows, cols, values):
    for ref, value in zip(refs, values):
        ref[rows, cols] = value


def block(j):
    return slice(NB * j, NB * (j + 1))


def gram(x_ref, rows, cols, same):
    n = x_ref.shape[0]
    out = mm(x_ref[:, rows], x_ref[:, cols], ((0,), (0,))) * (1.0 / n)
    if not same:
        return out
    row = lax.broadcasted_iota(jnp.int32, out.shape, 0)
    col = lax.broadcasted_iota(jnp.int32, out.shape, 1)
    return out + jnp.where(row == col, F32(0.001), F32(0))


def factor(a_ref, u_refs, w_ref, beside):
    half = a_ref.shape[0]
    count = half // NB
    head = a_ref[block(0), block(0)]
    tasks = []
    for j in range(count):
        w = inverse_factor(head, tasks + beside(j))
        w_ref[block(j), :] = w
        if j + 1 == count:
            return
        u = three(joined(three(w), three(a_ref[block(j), block(j + 1)]), 1, 0))
        put(u_refs, block(j), block(j + 1), u)
        head = a_ref[block(j + 1), block(j + 1)] - joined(u, u, 0, 0)
        tasks = []
        if j + 2 < count:
            far = slice(NB * (j + 2), half)

            def row(j=j, far=far):
                w = three(w_ref[block(j), :])
                put(u_refs, block(j), far, three(mm6(w, three(a_ref[block(j), far]), ((1,), (0,)))))

            def next_row(j=j, far=far):
                a_ref[block(j + 1), far] = a_ref[block(j + 1), far] - mm6(
                    parts(u_refs, block(j), block(j + 1)), parts(u_refs, block(j), far), ((0,), (0,))
                )

            def others(b, j=j):
                to = slice(NB * b, half)
                a_ref[block(b), to] = a_ref[block(b), to] - mm6(
                    parts(u_refs, block(j), block(b)), parts(u_refs, block(j), to), ((0,), (0,))
                )

            tasks = [row, next_row] + [lambda b=b, f=others: f(b) for b in range(j + 2, count)]


def pair_tasks(q, x_ref, u_refs, w_ref, wp_refs, b_refs, b_at):
    first, second = block(2 * q), block(2 * q + 1)
    both = slice(first.start, second.stop)
    above = slice(0, first.start)
    n = x_ref.shape[0]

    def joint():
        top, low = w_ref[first, :], three(w_ref[second, :])
        across = joined(parts(u_refs, first, second), three(top), 0, 0)
        across = joined(low, three(across), 1, 0)
        rows = jnp.concatenate([top, jnp.zeros_like(top)], axis=1)
        rows = jnp.concatenate([rows, jnp.concatenate([-across, w_ref[second, :]], axis=1)], axis=0)
        wp_refs[0][...], wp_refs[1][...] = two(rows)

    def columns(r):
        rows = slice(r, r + 256)
        rest = x_ref[rows, both].astype(F32)
        if q:
            held = tuple(ref[rows, slice(at, at + first.start)] for ref, at in zip(b_refs, b_at))
            rest = rest - mm3(held, parts(u_refs[:2], above, both), ((1,), (0,)))
        new = two(mm3(two(rest), (wp_refs[0][...], wp_refs[1][...]), ((1,), (1,))))
        for ref, at, value in zip(b_refs, b_at, new):
            ref[rows, slice(at + both.start, at + both.stop)] = value

    return [joint] + [lambda r=r: columns(r) for r in range(0, n, 256)]


def first_kernel(x_ref, *refs):
    out, held, (a_ref, wh_ref, wm_ref, sems) = refs[:6], refs[6:12], refs[12:]
    u_refs, b_refs, w_ref = held[:3], held[3:5], held[5]
    half = x_ref.shape[1]
    copies = [pltpu.make_async_copy(a, b, sems.at[i]) for i, (a, b) in enumerate(zip(held, out))]
    far = slice(NB, half)
    a_ref[block(0), block(0)] = gram(x_ref, block(0), block(0), True)

    def top():
        a_ref[block(0), far] = gram(x_ref, block(0), far, False)

    def rest():
        a_ref[far, far] = gram(x_ref, far, far, True)

    def beside(j):
        if j == 0:
            return [top, rest]
        if j == 2:
            return pair_tasks(0, x_ref, u_refs, w_ref, (wh_ref, wm_ref), b_refs, (0, 0))
        if j == half // NB - 1:
            for copy in copies[:5]:
                copy.start()
        return []

    factor(a_ref, u_refs, w_ref, beside)
    copies[5].start()
    for copy in copies:
        copy.wait()


def second_kernel(place_ref, *refs):
    given, (rows_ref, give_ref, keep_ref), held, rest = refs[:9], refs[9:12], refs[12:19], refs[19:]
    basis_ref, mid_ref, right_ref = rest[:3]
    u_refs, v_refs, wp_refs = rest[3:6], rest[6:9], rest[9:11]
    w_ref, a_ref, x_ref, moved_ref, sems = rest[11:]
    x2_ref, x1_ref, w1_ref, *u1_refs = held[:6]
    mixed_ref = held[6]
    n, half = x2_ref.shape
    count = half // NB
    first_pair = slice(0, 2 * NB)
    targets = (*held[:6], basis_ref.at[:, first_pair], mid_ref.at[:, first_pair], mixed_ref)
    copies = [pltpu.make_async_copy(a, b, sems.at[i]) for i, (a, b) in enumerate(zip(given, targets))]
    for copy in copies:
        copy.start()
    for copy in copies[:6]:
        copy.wait()
    far = slice(NB, half)

    def across(i, cols):
        acc = mm(x1_ref[:, block(i)], x2_ref[:, cols], ((0,), (0,))) * (1.0 / n)
        if i:
            above = slice(0, NB * i)
            acc = acc - mm6(parts(u1_refs, above, block(i)), parts(v_refs, above, cols), ((0,), (0,)))
        w = three(w1_ref[block(i), :])
        put(v_refs, block(i), cols, three(mm6(w, three(acc), ((1,), (0,)))))

    def left_over(rows, cols, same):
        every = slice(0, half)
        taken = mm6(parts(v_refs, every, rows), parts(v_refs, every, cols), ((0,), (0,)))
        a_ref[rows, cols] = gram(x2_ref, rows, cols, same) - taken

    for i in range(count):
        across(i, block(0))
    left_over(block(0), block(0), True)

    def arrive():
        copies[6].wait()
        copies[7].wait()

    def update(r):
        rows = slice(r, r + 256)
        held = (basis_ref[rows, :half], mid_ref[rows, :])
        x_ref[rows, :] = x2_ref[rows, :].astype(F32) - mm3(
            held, tuple(ref[...] for ref in v_refs[:2]), ((1,), (0,))
        )

    def move(r, cols):
        rows = slice(r, r + 256)
        moved_ref[rows, cols] = mm(mixed_ref[rows, :], basis_ref[:, cols], ((1,), (0,))).astype(BF16)

    chunks = range(0, n, 256)
    early, late = slice(0, half), slice(half, n)
    left_side = (x1_ref, u1_refs, w1_ref, wp_refs, (basis_ref, mid_ref), (0, 0))
    right_side = (x_ref, u_refs, w_ref, wp_refs, (basis_ref, right_ref), (half, 0))

    def beside(j):
        if j == 0:
            tasks = [lambda i=i: across(i, far) for i in range(count)]
            tasks.append(lambda: left_over(block(0), far, False))
            for b in range(1, count):
                tasks.append(lambda b=b: left_over(block(b), block(b), True))
                if b + 1 < count:
                    tasks.append(lambda b=b: left_over(block(b), slice(NB * (b + 1), half), False))
            return tasks
        if j == 1:
            return [arrive] + pair_tasks(1, *left_side)
        if j == 2:
            return [lambda r=r: update(r) for r in chunks]
        return [copies[8].wait] + pair_tasks(0, *right_side) + [lambda r=r: move(r, early) for r in chunks]

    factor(a_ref, u_refs, w_ref, beside)
    for task in pair_tasks(1, *right_side):
        task()
    me, core = place_ref[0], place_ref[1]
    own = rows_ref.shape[0]
    rows_ref[...] = basis_ref[pl.ds(pl.multiple_of(me * own, own), own), :]
    moved_ref[:, late] = mm(mixed_ref[...], basis_ref[:, late], ((1,), (0,))).astype(BF16)
    for ref, side in ((give_ref, 1 - core), (keep_ref, core)):
        cols = moved_ref[:, pl.ds(pl.multiple_of(side * half, half), half)]
        ref[...] = (mm(basis_ref[...], cols, ((0,), (0,))) * (1.0 / n)).astype(BF16)


VMEM = pl.BlockSpec(memory_space=pltpu.VMEM)
SMEM = pl.BlockSpec(memory_space=pltpu.SMEM)
HBM = pl.BlockSpec(memory_space=pltpu.HBM)


def basis_and_rotation(x1, x2, mixed, place, own):
    n, half = x1.shape
    sds = jax.ShapeDtypeStruct
    tall, square = sds((n, half), BF16), sds((half, half), BF16)
    pair, strip = sds((n, 2 * NB), BF16), sds((half, NB), F32)
    params = pltpu.CompilerParams(vmem_limit_bytes=60 * 2**20)
    a, wp = pltpu.VMEM((half, half), F32), pltpu.VMEM((2 * NB, 2 * NB), BF16)
    out = [square, square, square, pair, pair, strip]
    uh, um, ul, bh, bm, w = pl.pallas_call(
        first_kernel,
        out_shape=out,
        in_specs=[VMEM],
        out_specs=[HBM] * len(out),
        scratch_shapes=[pltpu.VMEM(s.shape, s.dtype) for s in out]
        + [a, wp, wp, pltpu.SemaphoreType.DMA((len(out),))],
        compiler_params=params,
    )(x1)
    operands = (x2, x1, w, uh, um, ul, bh, bm, mixed)
    waiting = operands[:6] + operands[8:]
    return pl.pallas_call(
        second_kernel,
        out_shape=[sds((own, n), BF16), tall, tall],
        in_specs=[SMEM] + [HBM] * len(operands),
        out_specs=[VMEM] * 3,
        scratch_shapes=[pltpu.VMEM(s.shape, s.dtype) for s in waiting]
        + [pltpu.VMEM((n, n), BF16), pltpu.VMEM((n, half), BF16), pltpu.VMEM((n, half), BF16)]
        + [pltpu.VMEM((half, half), BF16)] * 6
        + [wp, wp, pltpu.VMEM((half, NB), F32), a, pltpu.VMEM((n, half), F32)]
        + [pltpu.VMEM((n, n), BF16), pltpu.SemaphoreType.DMA((len(operands),))],
        compiler_params=params,
    )(place, *operands)


def sigma_kernel(
    coef_ref, dim_ref, psi_ref, left_hbm, right_hbm, sent_ref, denom_ref,
    app_ref, left_ref, right_ref, sems,
):
    n = psi_ref.shape[0]
    step = 256
    count = left_ref.shape[0]
    pairs = range(count)
    dim = dim_ref[0]
    blocks = [(p, slice(r, r + n // 2)) for p in pairs for r in (0, n // 2)]

    def fetch(source, held, at):
        return [
            pltpu.make_async_copy(source.at[0, p, rows, :], held.at[p, rows, :], sems.at[at, i])
            for i, (p, rows) in enumerate(blocks)
        ]

    lefts, rights = fetch(left_hbm, left_ref, 0), fetch(right_hbm, right_ref, 1)
    queue = lefts + rights
    ahead = 2
    for copy in queue[:ahead]:
        copy.start()
    for i, (copy, (p, rows)) in enumerate(zip(lefts, blocks)):
        copy.wait()
        for following in queue[ahead + 2 * i : ahead + 2 * i + 2]:
            following.start()
        app_ref[p, rows, :] = (
            coef_ref[p] * mm(left_ref[p, rows, :], psi_ref[...], ((1,), (0,)))
        ).astype(BF16)
    for copy in rights:
        copy.wait()
    row = lax.broadcasted_iota(jnp.int32, (n, step), 0)
    numer, denom = F32(0), F32(0)
    for c in range(0, n, step):
        cols = slice(c, c + step)
        total = mm(app_ref[0], right_ref[0, cols, :], ((1,), (1,)))
        for p in pairs[1:]:
            total = total + mm(app_ref[p], right_ref[p, cols, :], ((1,), (1,)))
        col = lax.broadcasted_iota(jnp.int32, (n, step), 1) + c
        total = jnp.where((row < dim) & (col < dim), total, F32(0))
        psi = psi_ref[:, cols].astype(F32)
        numer = numer + jnp.sum(psi * total)
        denom = denom + jnp.sum(psi * psi)
        sent_ref[:, cols] = total.astype(BF16)
    lane = lax.broadcasted_iota(jnp.int32, (n, NB), 1)
    numer = jnp.full((n, NB), numer, F32)
    high, mid, low = (part.astype(F32) for part in three(numer))
    tail = jnp.where(lane == 0, high, jnp.where(lane == 1, mid, jnp.where(lane == 2, low, F32(0))))
    sent_ref[:, n:] = tail.astype(BF16)
    denom_ref[0] = denom


def sigma_part(coef, dim, psi, left_ops, right_ops):
    n = psi.shape[0]
    sds = jax.ShapeDtypeStruct
    return pl.pallas_call(
        sigma_kernel,
        out_shape=[sds((n, n + NB), BF16), sds((1,), F32)],
        in_specs=[SMEM, SMEM, VMEM, HBM, HBM],
        out_specs=[VMEM, SMEM],
        scratch_shapes=[pltpu.VMEM(left_ops.shape[1:], BF16)] * 3
        + [pltpu.SemaphoreType.DMA((2, 2 * left_ops.shape[1]))],
        compiler_params=pltpu.CompilerParams(vmem_limit_bytes=46 * 2**20),
    )(coef, dim, psi, left_ops, right_ops)


def from_everyone(x, axis):
    count = lax.axis_size(axis)
    return lax.all_to_all(jnp.broadcast_to(x[None], (count, *x.shape)), axis, 0, 0, tiled=True)


def rows_of_all(x):
    got = from_everyone(x, OPS)
    return got.reshape(-1, got.shape[-1])


def to_owners(x):
    tiles = x.reshape(lax.axis_size(OPS), -1, x.shape[-1])
    return lax.all_to_all(tiles, OPS, 0, 0, tiled=True).astype(F32)


def shards(wavefunction, diag_scale, sector_dims, left_ops, right_ops, weight_index, weight_table):
    psi_local = wavefunction[0]
    rows_dev, order_k = psi_local.shape
    half = order_k // 2
    me = lax.axis_index(OPS)
    dim = sector_dims[0]
    live = jnp.arange(order_k) < dim
    row_live = me * rows_dev + jnp.arange(rows_dev) < dim
    mine = jnp.where(row_live[:, None] & live[None, :], psi_local, BF16(0))
    psi = rows_of_all(mine)
    onehot = weight_index[0][:, None] == jnp.arange(weight_table.shape[0])[None, :]
    coef = jnp.sum(jnp.where(onehot, weight_table[None, :], F32(0)), axis=1)
    mixed = coef[0] * left_ops[0, 0].astype(F32)
    for p in range(1, left_ops.shape[1]):
        mixed = mixed + coef[p] * left_ops[0, p].astype(F32)
    psi, mixed = lax.optimization_barrier((psi, mixed.astype(BF16)))
    sent, denom = sigma_part(coef, sector_dims, psi, left_ops, right_ops)
    arrived = to_owners(sent)
    sigma = jnp.sum(arrived[:, :, :order_k], axis=0)
    energy = jnp.sum(arrived[:, 0, order_k:]) / denom[0]
    old = mine.astype(F32)
    update = (old + (sigma - energy * old) / diag_scale[0]).astype(BF16)
    x = [rows_of_all(update[:, h]) for h in (slice(0, half), slice(half, order_k))]
    core = lax.axis_index("sector") % 2
    place = jnp.stack([me, core]).astype(jnp.int32)
    basis_local, give, keep = basis_and_rotation(*x, mixed, place, rows_dev)

    def swapped(values, bits):
        count = lax.axis_size("sector")
        return lax.ppermute(values, "sector", [(i, i ^ bits) for i in range(count)])

    kept = (keep.astype(F32) + swapped(give, 1).astype(F32)).astype(BF16)
    owned = jnp.sum(to_owners(kept), axis=0).astype(BF16)
    near, far, cross = (swapped(owned, bits).astype(F32) for bits in (1, 2, 3))
    own, other = owned.astype(F32) + far, near + cross
    next_rows = jnp.concatenate(
        [jnp.where(core == 0, own, other), jnp.where(core == 0, other, own)], axis=1
    )
    return (basis_local[None], jnp.reshape(energy, (1,)), next_rows)


def solution(mesh):
    split = Mesh(
        mesh.devices.reshape(mesh.shape["sector"], 4, 4, 2), ("sector", "ops_0", "ops_1", "ops_2")
    )
    in_specs = (
        P("sector", OPS, None),
        P("sector", OPS, None),
        P("sector"),
        P("sector", OPS, None, None),
        P("sector", OPS, None, None),
        P("sector", OPS),
        P(),
    )
    out_specs = (P("sector", OPS, None), P("sector"), P(OPS, None))
    return jax.shard_map(
        shards, mesh=split, in_specs=in_specs, out_specs=out_specs, check_vma=False
    )
```

```python
import jax
import jax.numpy as jnp
from jax import lax
from jax.experimental import pallas as pl
from jax.experimental.pallas import tpu as pltpu
from jax.sharding import Mesh
from jax.sharding import PartitionSpec as P

OPS = ("ops_0", "ops_1", "ops_2")
F32, BF16 = jnp.float32, jnp.bfloat16
NB = 128


def two(x):
    hi = x.astype(BF16)
    return hi, (x - hi.astype(F32)).astype(BF16)


def three(x):
    hi = x.astype(BF16)
    rest = x - hi.astype(F32)
    mid = rest.astype(BF16)
    return hi, mid, (rest - mid.astype(F32)).astype(BF16)


def mm(a, b, dims):
    return lax.dot_general(a, b, (dims, ((), ())), preferred_element_type=F32)


def mm6(a, b, dims):
    (ah, am, al), (bh, bm, bl) = a, b
    small = mm(al, bh, dims) + mm(ah, bl, dims) + mm(am, bm, dims)
    return small + (mm(am, bh, dims) + mm(ah, bm, dims)) + mm(ah, bh, dims)


def mm3(a, b, dims):
    (ah, al), (bh, bl) = a, b
    return mm(al, bh, dims) + mm(ah, bl, dims) + mm(ah, bh, dims)


def wide(x):
    return jnp.broadcast_to(x, (8, NB))


def stacked(rows):
    at = lax.broadcasted_iota(jnp.int32, (8, NB), 0)
    out = rows[0]
    for i in range(1, 8):
        out = jnp.where(at == i, rows[i], out)
    return out


def inv_sqrt(d):
    q = lax.rsqrt(d)
    return q * (1.5 - 0.5 * d * (q * q))


def inverse_factor(block, tasks=()):
    tasks = list(tasks)
    slots = len(tasks)
    panels = NB // 8
    a = [block[8 * i : 8 * i + 8] for i in range(panels)]
    row = lax.broadcasted_iota(jnp.int32, (NB, NB), 0)
    col = lax.broadcasted_iota(jnp.int32, (NB, NB), 1)
    eye = jnp.where(row == col, F32(1), F32(0))
    e = [eye[8 * i : 8 * i + 8] for i in range(panels)]
    done = []
    for p in range(panels):
        cols = [wide(a[p][:, 8 * p + j : 8 * p + j + 1]) for j in range(8)]
        s = {(i, j): wide(cols[j][i : i + 1]) for j in range(8) for i in range(j, 8)}
        u = [wide(a[p][i : i + 1]) for i in range(8)]
        w = [wide(e[p][i : i + 1]) for i in range(8)]
        last = p == panels - 1
        ahead = range(p + 1, min(p + 3, panels))
        v = {t: [wide(a[t][:, 8 * p + j : 8 * p + j + 1]) for j in range(8)] for t in ahead}
        us, ws = [], []
        for k in range(0, 8, 2):
            d0, c, d1 = s[k, k], s[k + 1, k], s[k + 1, k + 1]
            det = d0 * d1 - c * c
            rd = pl.reciprocal(det, approx=True)
            fix = 2.0 - det * rd
            n0 = {i: s[i, k] * d1 - s[i, k + 1] * c for i in range(k + 2, 8)}
            n1 = {i: s[i, k + 1] * d0 - s[i, k] * c for i in range(k + 2, 8)}
            soon = [(i, j) for j in range(k + 2, 4 + k) for i in range(j, 4 + k)] if k < 6 else []
            for i, j in soon:
                taken = n0[i] * s[j, k] + n1[i] * s[j, k + 1]
                s[i, j] = s[i, j] - (taken * rd) * fix
            rd = rd * fix
            f0 = {i: n0[i] * rd for i in n0}
            f1 = {i: n1[i] * rd for i in n1}
            for i in range(k + 2, 8):
                for j in range(k + 2, i + 1):
                    if (i, j) not in soon:
                        s[i, j] = s[i, j] - (f0[i] * s[j, k] + f1[i] * s[j, k + 1])
            r0 = pl.reciprocal(d0, approx=True)
            r0 = r0 * (2.0 - d0 * r0)
            q0, q1 = inv_sqrt(d0), inv_sqrt(det * r0)
            g = c * r0

            def swept(rows):
                for i in range(k + 2, 8):
                    rows[i] = rows[i] - (f0[i] * rows[k] + f1[i] * rows[k + 1])
                return rows[k] * q0, (rows[k + 1] - g * rows[k]) * q1

            for t in ahead:
                v0, v1 = v[t][k], v[t][k + 1]
                g0, g1 = (v0 * d1 - v1 * c) * rd, (v1 * d0 - v0 * c) * rd
                swept(v[t])
                a[t] = a[t] - (g0 * u[k] + g1 * u[k + 1])
                e[t] = e[t] - (g0 * w[k] + g1 * w[k + 1])
            ws.extend(swept(w))
            if not last:
                us.extend(swept(u))
        while tasks and (slots - len(tasks)) * (panels - 3) < slots * p:
            tasks.pop(0)()
        wp = stacked(ws)
        done.append(wp)
        if last:
            break
        if ahead.stop == panels:
            continue
        up = stacked(us)
        both = jnp.concatenate([up, wp], axis=1)
        h = both.astype(BF16).astype(F32)
        m = (both - h).astype(BF16).astype(F32)
        t = both - h - m
        left = jnp.concatenate([x[:, :NB] for x in (h, h, m, m, h, t)], axis=0).astype(BF16)
        right = jnp.concatenate([h, m, h, m, t, h], axis=0).astype(BF16)
        out = mm(left, right, ((0,), (0,)))
        for i in range(ahead.stop, panels):
            a[i] = a[i] - out[8 * i : 8 * i + 8, :NB]
            e[i] = e[i] - out[8 * i : 8 * i + 8, NB:]
    return jnp.concatenate(done, axis=0)


def joined(a, b, a_dim, b_dim):
    (ah, am, al), (bh, bm, bl) = a, b
    left = jnp.concatenate([al, ah, am, am, ah, ah], axis=a_dim)
    right = jnp.concatenate([bh, bl, bm, bh, bm, bh], axis=b_dim)
    return mm(left, right, ((a_dim,), (b_dim,)))


def parts(refs, rows, cols):
    return tuple(ref[rows, cols] for ref in refs)


def put(refs, rows, cols, values):
    for ref, value in zip(refs, values):
        ref[rows, cols] = value


def block(j):
    return slice(NB * j, NB * (j + 1))


def gram(x_ref, rows, cols, same):
    n = x_ref.shape[0]
    out = mm(x_ref[:, rows], x_ref[:, cols], ((0,), (0,))) * (1.0 / n)
    if not same:
        return out
    row = lax.broadcasted_iota(jnp.int32, out.shape, 0)
    col = lax.broadcasted_iota(jnp.int32, out.shape, 1)
    return out + jnp.where(row == col, F32(0.001), F32(0))


def factor(a_ref, u_refs, w_ref, beside):
    half = a_ref.shape[0]
    count = half // NB
    head = a_ref[block(0), block(0)]
    tasks = []
    for j in range(count):
        w = inverse_factor(head, tasks + beside(j))
        w_ref[block(j), :] = w
        if j + 1 == count:
            return
        u = three(joined(three(w), three(a_ref[block(j), block(j + 1)]), 1, 0))
        put(u_refs, block(j), block(j + 1), u)
        head = a_ref[block(j + 1), block(j + 1)] - joined(u, u, 0, 0)
        tasks = []
        if j + 2 < count:
            far = slice(NB * (j + 2), half)

            def row(j=j, far=far):
                w = three(w_ref[block(j), :])
                put(u_refs, block(j), far, three(mm6(w, three(a_ref[block(j), far]), ((1,), (0,)))))

            def next_row(j=j, far=far):
                a_ref[block(j + 1), far] = a_ref[block(j + 1), far] - mm6(
                    parts(u_refs, block(j), block(j + 1)), parts(u_refs, block(j), far), ((0,), (0,))
                )

            def others(b, j=j):
                to = slice(NB * b, half)
                a_ref[block(b), to] = a_ref[block(b), to] - mm6(
                    parts(u_refs, block(j), block(b)), parts(u_refs, block(j), to), ((0,), (0,))
                )

            tasks = [row, next_row] + [lambda b=b, f=others: f(b) for b in range(j + 2, count)]


def pair_tasks(q, x_ref, u_refs, w_ref, wp_refs, b_refs, b_at):
    first, second = block(2 * q), block(2 * q + 1)
    both = slice(first.start, second.stop)
    above = slice(0, first.start)
    n = x_ref.shape[0]

    def joint():
        top, low = w_ref[first, :], three(w_ref[second, :])
        across = joined(parts(u_refs, first, second), three(top), 0, 0)
        across = joined(low, three(across), 1, 0)
        rows = jnp.concatenate([top, jnp.zeros_like(top)], axis=1)
        rows = jnp.concatenate([rows, jnp.concatenate([-across, w_ref[second, :]], axis=1)], axis=0)
        wp_refs[0][...], wp_refs[1][...] = two(rows)

    def columns(r):
        rows = slice(r, r + 256)
        rest = x_ref[rows, both].astype(F32)
        if q:
            held = tuple(ref[rows, slice(at, at + first.start)] for ref, at in zip(b_refs, b_at))
            rest = rest - mm3(held, parts(u_refs[:2], above, both), ((1,), (0,)))
        new = two(mm3(two(rest), (wp_refs[0][...], wp_refs[1][...]), ((1,), (1,))))
        for ref, at, value in zip(b_refs, b_at, new):
            ref[rows, slice(at + both.start, at + both.stop)] = value

    return [joint] + [lambda r=r: columns(r) for r in range(0, n, 256)]


def first_kernel(x_ref, *refs):
    out, held, (a_ref, wh_ref, wm_ref, sems) = refs[:6], refs[6:12], refs[12:]
    u_refs, b_refs, w_ref = held[:3], held[3:5], held[5]
    half = x_ref.shape[1]
    copies = [pltpu.make_async_copy(a, b, sems.at[i]) for i, (a, b) in enumerate(zip(held, out))]
    far = slice(NB, half)
    a_ref[block(0), block(0)] = gram(x_ref, block(0), block(0), True)

    def top():
        a_ref[block(0), far] = gram(x_ref, block(0), far, False)

    def rest():
        a_ref[far, far] = gram(x_ref, far, far, True)

    def beside(j):
        if j == 0:
            return [top, rest]
        if j == 2:
            return pair_tasks(0, x_ref, u_refs, w_ref, (wh_ref, wm_ref), b_refs, (0, 0))
        if j == half // NB - 1:
            for copy in copies[:5]:
                copy.start()
        return []

    factor(a_ref, u_refs, w_ref, beside)
    copies[5].start()
    for copy in copies:
        copy.wait()


def second_kernel(place_ref, *refs):
    given, (rows_ref, give_ref, keep_ref), held, rest = refs[:9], refs[9:12], refs[12:19], refs[19:]
    basis_ref, mid_ref, right_ref = rest[:3]
    u_refs, v_refs, wp_refs = rest[3:6], rest[6:9], rest[9:11]
    w_ref, a_ref, x_ref, moved_ref, sems = rest[11:]
    x2_ref, x1_ref, w1_ref, *u1_refs = held[:6]
    mixed_ref = held[6]
    n, half = x2_ref.shape
    count = half // NB
    first_pair = slice(0, 2 * NB)
    targets = (*held[:6], basis_ref.at[:, first_pair], mid_ref.at[:, first_pair], mixed_ref)
    copies = [pltpu.make_async_copy(a, b, sems.at[i]) for i, (a, b) in enumerate(zip(given, targets))]
    for copy in copies:
        copy.start()
    for copy in copies[:6]:
        copy.wait()
    far = slice(NB, half)

    def across(i, cols):
        acc = mm(x1_ref[:, block(i)], x2_ref[:, cols], ((0,), (0,))) * (1.0 / n)
        if i:
            above = slice(0, NB * i)
            acc = acc - mm6(parts(u1_refs, above, block(i)), parts(v_refs, above, cols), ((0,), (0,)))
        w = three(w1_ref[block(i), :])
        put(v_refs, block(i), cols, three(mm6(w, three(acc), ((1,), (0,)))))

    def left_over(rows, cols, same):
        every = slice(0, half)
        taken = mm6(parts(v_refs, every, rows), parts(v_refs, every, cols), ((0,), (0,)))
        a_ref[rows, cols] = gram(x2_ref, rows, cols, same) - taken

    for i in range(count):
        across(i, block(0))
    left_over(block(0), block(0), True)

    def arrive():
        copies[6].wait()
        copies[7].wait()

    def update(r):
        rows = slice(r, r + 256)
        held = (basis_ref[rows, :half], mid_ref[rows, :])
        x_ref[rows, :] = x2_ref[rows, :].astype(F32) - mm3(
            held, tuple(ref[...] for ref in v_refs[:2]), ((1,), (0,))
        )

    def move(r, cols):
        rows = slice(r, r + 256)
        moved_ref[rows, cols] = mm(mixed_ref[rows, :], basis_ref[:, cols], ((1,), (0,))).astype(BF16)

    chunks = range(0, n, 256)
    early, late = slice(0, half), slice(half, n)
    left_side = (x1_ref, u1_refs, w1_ref, wp_refs, (basis_ref, mid_ref), (0, 0))
    right_side = (x_ref, u_refs, w_ref, wp_refs, (basis_ref, right_ref), (half, 0))

    def beside(j):
        if j == 0:
            tasks = [lambda i=i: across(i, far) for i in range(count)]
            tasks.append(lambda: left_over(block(0), far, False))
            for b in range(1, count):
                tasks.append(lambda b=b: left_over(block(b), block(b), True))
                if b + 1 < count:
                    tasks.append(lambda b=b: left_over(block(b), slice(NB * (b + 1), half), False))
            return tasks
        if j == 1:
            return [arrive] + pair_tasks(1, *left_side)
        if j == 2:
            return [lambda r=r: update(r) for r in chunks]
        return [copies[8].wait] + pair_tasks(0, *right_side) + [lambda r=r: move(r, early) for r in chunks]

    factor(a_ref, u_refs, w_ref, beside)
    for task in pair_tasks(1, *right_side):
        task()
    me, core = place_ref[0], place_ref[1]
    own = rows_ref.shape[0]
    rows_ref[...] = basis_ref[pl.ds(pl.multiple_of(me * own, own), own), :]
    moved_ref[:, late] = mm(mixed_ref[...], basis_ref[:, late], ((1,), (0,))).astype(BF16)
    for ref, side in ((give_ref, 1 - core), (keep_ref, core)):
        cols = moved_ref[:, pl.ds(pl.multiple_of(side * half, half), half)]
        ref[...] = (mm(basis_ref[...], cols, ((0,), (0,))) * (1.0 / n)).astype(BF16)


VMEM = pl.BlockSpec(memory_space=pltpu.VMEM)
SMEM = pl.BlockSpec(memory_space=pltpu.SMEM)
HBM = pl.BlockSpec(memory_space=pltpu.HBM)


def basis_and_rotation(x1, x2, mixed, place, own):
    n, half = x1.shape
    sds = jax.ShapeDtypeStruct
    tall, square = sds((n, half), BF16), sds((half, half), BF16)
    pair, strip = sds((n, 2 * NB), BF16), sds((half, NB), F32)
    params = pltpu.CompilerParams(vmem_limit_bytes=60 * 2**20)
    a, wp = pltpu.VMEM((half, half), F32), pltpu.VMEM((2 * NB, 2 * NB), BF16)
    out = [square, square, square, pair, pair, strip]
    uh, um, ul, bh, bm, w = pl.pallas_call(
        first_kernel,
        out_shape=out,
        in_specs=[VMEM],
        out_specs=[HBM] * len(out),
        scratch_shapes=[pltpu.VMEM(s.shape, s.dtype) for s in out]
        + [a, wp, wp, pltpu.SemaphoreType.DMA((len(out),))],
        compiler_params=params,
    )(x1)
    operands = (x2, x1, w, uh, um, ul, bh, bm, mixed)
    waiting = operands[:6] + operands[8:]
    return pl.pallas_call(
        second_kernel,
        out_shape=[sds((own, n), BF16), tall, tall],
        in_specs=[SMEM] + [HBM] * len(operands),
        out_specs=[VMEM] * 3,
        scratch_shapes=[pltpu.VMEM(s.shape, s.dtype) for s in waiting]
        + [pltpu.VMEM((n, n), BF16), pltpu.VMEM((n, half), BF16), pltpu.VMEM((n, half), BF16)]
        + [pltpu.VMEM((half, half), BF16)] * 6
        + [wp, wp, pltpu.VMEM((half, NB), F32), a, pltpu.VMEM((n, half), F32)]
        + [pltpu.VMEM((n, n), BF16), pltpu.SemaphoreType.DMA((len(operands),))],
        compiler_params=params,
    )(place, *operands)


def sigma_kernel(
    coef_ref, dim_ref, psi_ref, left_hbm, right_hbm, sent_ref, denom_ref,
    app_ref, left_ref, right_ref, sems,
):
    n = psi_ref.shape[0]
    step = 256
    count = left_ref.shape[0]
    pairs = range(count)
    dim = dim_ref[0]
    blocks = [(p, slice(r, r + n // 2)) for p in pairs for r in (0, n // 2)]

    def fetch(source, held, at):
        return [
            pltpu.make_async_copy(source.at[0, p, rows, :], held.at[p, rows, :], sems.at[at, i])
            for i, (p, rows) in enumerate(blocks)
        ]

    lefts, rights = fetch(left_hbm, left_ref, 0), fetch(right_hbm, right_ref, 1)
    queue = lefts + rights
    ahead = 2
    for copy in queue[:ahead]:
        copy.start()
    for i, (copy, (p, rows)) in enumerate(zip(lefts, blocks)):
        copy.wait()
        for following in queue[ahead + 2 * i : ahead + 2 * i + 2]:
            following.start()
        app_ref[p, rows, :] = mm(left_ref[p, rows, :], psi_ref[...], ((1,), (0,))).astype(BF16)
    for copy in rights:
        copy.wait()
    row = lax.broadcasted_iota(jnp.int32, (n, step), 0)
    numer, denom = F32(0), F32(0)
    for c in range(0, n, step):
        cols = slice(c, c + step)
        total = coef_ref[0] * mm(app_ref[0], right_ref[0, cols, :], ((1,), (1,)))
        for p in pairs[1:]:
            total = total + coef_ref[p] * mm(app_ref[p], right_ref[p, cols, :], ((1,), (1,)))
        col = lax.broadcasted_iota(jnp.int32, (n, step), 1) + c
        total = jnp.where((row < dim) & (col < dim), total, F32(0))
        psi = psi_ref[:, cols].astype(F32)
        numer = numer + jnp.sum(psi * total)
        denom = denom + jnp.sum(psi * psi)
        sent_ref[:, cols] = total.astype(BF16)
    lane = lax.broadcasted_iota(jnp.int32, (n, NB), 1)
    numer = jnp.full((n, NB), numer, F32)
    high, mid, low = (part.astype(F32) for part in three(numer))
    tail = jnp.where(lane == 0, high, jnp.where(lane == 1, mid, jnp.where(lane == 2, low, F32(0))))
    sent_ref[:, n:] = tail.astype(BF16)
    denom_ref[0] = denom


def sigma_part(coef, dim, psi, left_ops, right_ops):
    n = psi.shape[0]
    sds = jax.ShapeDtypeStruct
    return pl.pallas_call(
        sigma_kernel,
        out_shape=[sds((n, n + NB), BF16), sds((1,), F32)],
        in_specs=[SMEM, SMEM, VMEM, HBM, HBM],
        out_specs=[VMEM, SMEM],
        scratch_shapes=[pltpu.VMEM(left_ops.shape[1:], BF16)] * 3
        + [pltpu.SemaphoreType.DMA((2, 2 * left_ops.shape[1]))],
        compiler_params=pltpu.CompilerParams(vmem_limit_bytes=46 * 2**20),
    )(coef, dim, psi, left_ops, right_ops)


def from_everyone(x, axis):
    count = lax.axis_size(axis)
    return lax.all_to_all(jnp.broadcast_to(x[None], (count, *x.shape)), axis, 0, 0, tiled=True)


def rows_of_all(x):
    got = from_everyone(x, OPS)
    return got.reshape(-1, got.shape[-1])


def to_owners(x):
    tiles = x.reshape(lax.axis_size(OPS), -1, x.shape[-1])
    return lax.all_to_all(tiles, OPS, 0, 0, tiled=True).astype(F32)


def shards(wavefunction, diag_scale, sector_dims, left_ops, right_ops, weight_index, weight_table):
    psi_local = wavefunction[0]
    rows_dev, order_k = psi_local.shape
    half = order_k // 2
    me = lax.axis_index(OPS)
    dim = sector_dims[0]
    live = jnp.arange(order_k) < dim
    row_live = me * rows_dev + jnp.arange(rows_dev) < dim
    mine = jnp.where(row_live[:, None] & live[None, :], psi_local, BF16(0))
    psi = rows_of_all(mine)
    onehot = weight_index[0][:, None] == jnp.arange(weight_table.shape[0])[None, :]
    coef = jnp.sum(jnp.where(onehot, weight_table[None, :], F32(0)), axis=1)
    mixed = coef[0] * left_ops[0, 0].astype(F32)
    for p in range(1, left_ops.shape[1]):
        mixed = mixed + coef[p] * left_ops[0, p].astype(F32)
    psi, mixed = lax.optimization_barrier((psi, mixed.astype(BF16)))
    sent, denom = sigma_part(coef, sector_dims, psi, left_ops, right_ops)
    arrived = to_owners(sent)
    sigma = jnp.sum(arrived[:, :, :order_k], axis=0)
    energy = jnp.sum(arrived[:, 0, order_k:]) / denom[0]
    old = mine.astype(F32)
    update = (old + (sigma - energy * old) / diag_scale[0]).astype(BF16)
    x = [rows_of_all(update[:, h]) for h in (slice(0, half), slice(half, order_k))]
    core = lax.axis_index("sector") % 2
    place = jnp.stack([me, core]).astype(jnp.int32)
    basis_local, give, keep = basis_and_rotation(*x, mixed, place, rows_dev)

    def swapped(values, bits):
        count = lax.axis_size("sector")
        return lax.ppermute(values, "sector", [(i, i ^ bits) for i in range(count)])

    kept = (keep.astype(F32) + swapped(give, 1).astype(F32)).astype(BF16)
    owned = jnp.sum(to_owners(kept), axis=0).astype(BF16)
    near, far, cross = (swapped(owned, bits).astype(F32) for bits in (1, 2, 3))
    own, other = owned.astype(F32) + far, near + cross
    next_rows = jnp.concatenate(
        [jnp.where(core == 0, own, other), jnp.where(core == 0, other, own)], axis=1
    )
    return (basis_local[None], jnp.reshape(energy, (1,)), next_rows)


def solution(mesh):
    split = Mesh(
        mesh.devices.reshape(mesh.shape["sector"], 4, 4, 2), ("sector", "ops_0", "ops_1", "ops_2")
    )
    in_specs = (
        P("sector", OPS, None),
        P("sector", OPS, None),
        P("sector"),
        P("sector", OPS, None, None),
        P("sector", OPS, None, None),
        P("sector", OPS),
        P(),
    )
    out_specs = (P("sector", OPS, None), P("sector"), P(OPS, None))
    return jax.shard_map(
        shards, mesh=split, in_specs=in_specs, out_specs=out_specs, check_vma=False
    )
```

```python
import jax
import jax.numpy as jnp
from jax import lax
from jax.experimental import pallas as pl
from jax.experimental.pallas import tpu as pltpu
from jax.sharding import Mesh
from jax.sharding import PartitionSpec as P

OPS = ("ops_0", "ops_1", "ops_2")
F32, BF16 = jnp.float32, jnp.bfloat16
NB = 128


def two(x):
    hi = x.astype(BF16)
    return hi, (x - hi.astype(F32)).astype(BF16)


def three(x):
    hi = x.astype(BF16)
    rest = x - hi.astype(F32)
    mid = rest.astype(BF16)
    return hi, mid, (rest - mid.astype(F32)).astype(BF16)


def mm(a, b, dims):
    return lax.dot_general(a, b, (dims, ((), ())), preferred_element_type=F32)


def mm6(a, b, dims):
    (ah, am, al), (bh, bm, bl) = a, b
    small = mm(al, bh, dims) + mm(ah, bl, dims) + mm(am, bm, dims)
    return small + (mm(am, bh, dims) + mm(ah, bm, dims)) + mm(ah, bh, dims)


def mm3(a, b, dims):
    (ah, al), (bh, bl) = a, b
    return mm(al, bh, dims) + mm(ah, bl, dims) + mm(ah, bh, dims)


def wide(x):
    return jnp.broadcast_to(x, (8, NB))


def stacked(rows):
    at = lax.broadcasted_iota(jnp.int32, (8, NB), 0)
    out = rows[0]
    for i in range(1, 8):
        out = jnp.where(at == i, rows[i], out)
    return out


def inv_sqrt(d):
    q = lax.rsqrt(d)
    return q * (1.5 - 0.5 * d * (q * q))


def inverse_factor(block, tasks=()):
    tasks = list(tasks)
    slots = len(tasks)
    panels = NB // 8
    a = [block[8 * i : 8 * i + 8] for i in range(panels)]
    row = lax.broadcasted_iota(jnp.int32, (NB, NB), 0)
    col = lax.broadcasted_iota(jnp.int32, (NB, NB), 1)
    eye = jnp.where(row == col, F32(1), F32(0))
    e = [eye[8 * i : 8 * i + 8] for i in range(panels)]
    done = []
    for p in range(panels):
        cols = [wide(a[p][:, 8 * p + j : 8 * p + j + 1]) for j in range(8)]
        s = {(i, j): wide(cols[j][i : i + 1]) for j in range(8) for i in range(j, 8)}
        u = [wide(a[p][i : i + 1]) for i in range(8)]
        w = [wide(e[p][i : i + 1]) for i in range(8)]
        last = p == panels - 1
        ahead = range(p + 1, min(p + 3, panels))
        v = {t: [wide(a[t][:, 8 * p + j : 8 * p + j + 1]) for j in range(8)] for t in ahead}
        us, ws = [], []
        for k in range(0, 8, 2):
            d0, c, d1 = s[k, k], s[k + 1, k], s[k + 1, k + 1]
            det = d0 * d1 - c * c
            rd = pl.reciprocal(det, approx=True)
            fix = 2.0 - det * rd
            n0 = {i: s[i, k] * d1 - s[i, k + 1] * c for i in range(k + 2, 8)}
            n1 = {i: s[i, k + 1] * d0 - s[i, k] * c for i in range(k + 2, 8)}
            soon = [(i, j) for j in range(k + 2, 4 + k) for i in range(j, 4 + k)] if k < 6 else []
            for i, j in soon:
                taken = n0[i] * s[j, k] + n1[i] * s[j, k + 1]
                s[i, j] = s[i, j] - (taken * rd) * fix
            rd = rd * fix
            f0 = {i: n0[i] * rd for i in n0}
            f1 = {i: n1[i] * rd for i in n1}
            for i in range(k + 2, 8):
                for j in range(k + 2, i + 1):
                    if (i, j) not in soon:
                        s[i, j] = s[i, j] - (f0[i] * s[j, k] + f1[i] * s[j, k + 1])
            r0 = pl.reciprocal(d0, approx=True)
            r0 = r0 * (2.0 - d0 * r0)
            q0, q1 = inv_sqrt(d0), inv_sqrt(det * r0)
            g = c * r0

            def swept(rows):
                for i in range(k + 2, 8):
                    rows[i] = rows[i] - (f0[i] * rows[k] + f1[i] * rows[k + 1])
                return rows[k] * q0, (rows[k + 1] - g * rows[k]) * q1

            for t in ahead:
                v0, v1 = v[t][k], v[t][k + 1]
                g0, g1 = (v0 * d1 - v1 * c) * rd, (v1 * d0 - v0 * c) * rd
                swept(v[t])
                a[t] = a[t] - (g0 * u[k] + g1 * u[k + 1])
                e[t] = e[t] - (g0 * w[k] + g1 * w[k + 1])
            ws.extend(swept(w))
            if not last:
                us.extend(swept(u))
        while tasks and (slots - len(tasks)) * (panels - 3) < slots * p:
            tasks.pop(0)()
        wp = stacked(ws)
        done.append(wp)
        if last:
            break
        if ahead.stop == panels:
            continue
        up = stacked(us)
        both = jnp.concatenate([up, wp], axis=1)
        h = both.astype(BF16).astype(F32)
        m = (both - h).astype(BF16).astype(F32)
        t = both - h - m
        left = jnp.concatenate([x[:, :NB] for x in (h, h, m, m, h, t)], axis=0).astype(BF16)
        right = jnp.concatenate([h, m, h, m, t, h], axis=0).astype(BF16)
        out = mm(left, right, ((0,), (0,)))
        for i in range(ahead.stop, panels):
            a[i] = a[i] - out[8 * i : 8 * i + 8, :NB]
            e[i] = e[i] - out[8 * i : 8 * i + 8, NB:]
    return jnp.concatenate(done, axis=0)


def joined(a, b, a_dim, b_dim):
    (ah, am, al), (bh, bm, bl) = a, b
    left = jnp.concatenate([al, ah, am, am, ah, ah], axis=a_dim)
    right = jnp.concatenate([bh, bl, bm, bh, bm, bh], axis=b_dim)
    return mm(left, right, ((a_dim,), (b_dim,)))


def parts(refs, rows, cols):
    return tuple(ref[rows, cols] for ref in refs)


def put(refs, rows, cols, values):
    for ref, value in zip(refs, values):
        ref[rows, cols] = value


def block(j):
    return slice(NB * j, NB * (j + 1))


def gram(x_ref, rows, cols, same):
    n = x_ref.shape[0]
    out = mm(x_ref[:, rows], x_ref[:, cols], ((0,), (0,))) * (1.0 / n)
    if not same:
        return out
    row = lax.broadcasted_iota(jnp.int32, out.shape, 0)
    col = lax.broadcasted_iota(jnp.int32, out.shape, 1)
    return out + jnp.where(row == col, F32(0.001), F32(0))


def next_block(a_ref, u_refs, w_ref, j):
    half = a_ref.shape[0]
    count = half // NB
    u = three(joined(three(w_ref[block(j), :]), three(a_ref[block(j), block(j + 1)]), 1, 0))
    put(u_refs, block(j), block(j + 1), u)
    head = a_ref[block(j + 1), block(j + 1)] - joined(u, u, 0, 0)
    if j + 2 == count:
        return head, []
    far = slice(NB * (j + 2), half)

    def row():
        w = three(w_ref[block(j), :])
        put(u_refs, block(j), far, three(mm6(w, three(a_ref[block(j), far]), ((1,), (0,)))))

    def next_row():
        a_ref[block(j + 1), far] = a_ref[block(j + 1), far] - mm6(
            parts(u_refs, block(j), block(j + 1)), parts(u_refs, block(j), far), ((0,), (0,))
        )

    def others(b):
        to = slice(NB * b, half)
        a_ref[block(b), to] = a_ref[block(b), to] - mm6(
            parts(u_refs, block(j), block(b)), parts(u_refs, block(j), to), ((0,), (0,))
        )

    return head, [row, next_row] + [lambda b=b: others(b) for b in range(j + 2, count)]


def factor(a_ref, u_refs, w_ref, beside):
    count = a_ref.shape[0] // NB
    head = a_ref[block(0), block(0)]
    tasks = []
    for j in range(count):
        w_ref[block(j), :] = inverse_factor(head, tasks + beside(j))
        if j + 1 < count:
            head, tasks = next_block(a_ref, u_refs, w_ref, j)


def pair_tasks(q, x_ref, u_refs, w_ref, wp_refs, b_refs, b_at):
    first, second = block(2 * q), block(2 * q + 1)
    both = slice(first.start, second.stop)
    above = slice(0, first.start)
    n = x_ref.shape[0]

    def joint():
        top, low = w_ref[first, :], three(w_ref[second, :])
        across = joined(parts(u_refs, first, second), three(top), 0, 0)
        across = joined(low, three(across), 1, 0)
        rows = jnp.concatenate([top, jnp.zeros_like(top)], axis=1)
        rows = jnp.concatenate([rows, jnp.concatenate([-across, w_ref[second, :]], axis=1)], axis=0)
        wp_refs[0][...], wp_refs[1][...] = two(rows)

    def columns(r):
        rows = slice(r, r + 256)
        rest = x_ref[rows, both].astype(F32)
        if q:
            held = tuple(ref[rows, slice(at, at + first.start)] for ref, at in zip(b_refs, b_at))
            rest = rest - mm3(held, parts(u_refs[:2], above, both), ((1,), (0,)))
        new = two(mm3(two(rest), (wp_refs[0][...], wp_refs[1][...]), ((1,), (1,))))
        for ref, at, value in zip(b_refs, b_at, new):
            ref[rows, slice(at + both.start, at + both.stop)] = value

    return [joint] + [lambda r=r: columns(r) for r in range(0, n, 256)]


def first_kernel(x_ref, *refs):
    out, held, (a_ref, wh_ref, wm_ref, head_ref, sems) = refs[:6], refs[6:12], refs[12:]
    u_refs, b_refs, w_ref = held[:3], held[3:5], held[5]
    half = x_ref.shape[1]
    copies = [pltpu.make_async_copy(a, b, sems.at[i]) for i, (a, b) in enumerate(zip(held, out))]
    far = slice(NB, half)
    a_ref[block(0), block(0)] = gram(x_ref, block(0), block(0), True)

    def top():
        a_ref[block(0), far] = gram(x_ref, block(0), far, False)

    def rest():
        a_ref[far, far] = gram(x_ref, far, far, True)

    def after(j):
        if j == 0:
            top()
            rest()
        if j + 1 < half // NB:
            head, tasks = next_block(a_ref, u_refs, w_ref, j)
            head_ref[...] = head
            for task in tasks:
                task()
        if j == 1:
            for task in pair_tasks(0, x_ref, u_refs, w_ref, (wh_ref, wm_ref), b_refs, (0, 0)):
                task()
        if j == 2:
            for copy in copies[:5]:
                copy.start()

    head_ref[...] = a_ref[block(0), block(0)]

    def step(k, carry):
        w_ref[pl.ds(pl.multiple_of(k * NB, NB), NB), :] = inverse_factor(head_ref[...])
        for j in range(half // NB):
            pl.when(k == j)(lambda j=j: after(j))
        return carry

    lax.fori_loop(0, half // NB, step, 0)
    copies[5].start()
    for copy in copies:
        copy.wait()


def second_kernel(place_ref, *refs):
    given, (rows_ref, give_ref, keep_ref), held, rest = refs[:9], refs[9:12], refs[12:19], refs[19:]
    basis_ref, mid_ref, right_ref = rest[:3]
    u_refs, v_refs, wp_refs = rest[3:6], rest[6:9], rest[9:11]
    w_ref, a_ref, x_ref, moved_ref, sems = rest[11:]
    x2_ref, x1_ref, w1_ref, *u1_refs = held[:6]
    mixed_ref = held[6]
    n, half = x2_ref.shape
    count = half // NB
    first_pair = slice(0, 2 * NB)
    targets = (*held[:6], basis_ref.at[:, first_pair], mid_ref.at[:, first_pair], mixed_ref)
    copies = [pltpu.make_async_copy(a, b, sems.at[i]) for i, (a, b) in enumerate(zip(given, targets))]
    for copy in copies:
        copy.start()
    for copy in copies[:6]:
        copy.wait()
    far = slice(NB, half)

    def across(i, cols):
        acc = mm(x1_ref[:, block(i)], x2_ref[:, cols], ((0,), (0,))) * (1.0 / n)
        if i:
            above = slice(0, NB * i)
            acc = acc - mm6(parts(u1_refs, above, block(i)), parts(v_refs, above, cols), ((0,), (0,)))
        w = three(w1_ref[block(i), :])
        put(v_refs, block(i), cols, three(mm6(w, three(acc), ((1,), (0,)))))

    def left_over(rows, cols, same):
        every = slice(0, half)
        taken = mm6(parts(v_refs, every, rows), parts(v_refs, every, cols), ((0,), (0,)))
        a_ref[rows, cols] = gram(x2_ref, rows, cols, same) - taken

    for i in range(count):
        across(i, block(0))
    left_over(block(0), block(0), True)

    def arrive():
        copies[6].wait()
        copies[7].wait()

    def update(r):
        rows = slice(r, r + 256)
        held = (basis_ref[rows, :half], mid_ref[rows, :])
        x_ref[rows, :] = x2_ref[rows, :].astype(F32) - mm3(
            held, tuple(ref[...] for ref in v_refs[:2]), ((1,), (0,))
        )

    def move(r, cols):
        rows = slice(r, r + 256)
        moved_ref[rows, cols] = mm(mixed_ref[rows, :], basis_ref[:, cols], ((1,), (0,))).astype(BF16)

    chunks = range(0, n, 256)
    early, late = slice(0, half), slice(half, n)
    left_side = (x1_ref, u1_refs, w1_ref, wp_refs, (basis_ref, mid_ref), (0, 0))
    right_side = (x_ref, u_refs, w_ref, wp_refs, (basis_ref, right_ref), (half, 0))

    def beside(j):
        if j == 0:
            tasks = [lambda i=i: across(i, far) for i in range(count)]
            tasks.append(lambda: left_over(block(0), far, False))
            for b in range(1, count):
                tasks.append(lambda b=b: left_over(block(b), block(b), True))
                if b + 1 < count:
                    tasks.append(lambda b=b: left_over(block(b), slice(NB * (b + 1), half), False))
            return tasks
        if j == 1:
            return [arrive] + pair_tasks(1, *left_side)
        if j == 2:
            return [lambda r=r: update(r) for r in chunks]
        return [copies[8].wait] + pair_tasks(0, *right_side) + [lambda r=r: move(r, early) for r in chunks]

    factor(a_ref, u_refs, w_ref, beside)
    for task in pair_tasks(1, *right_side):
        task()
    me, core = place_ref[0], place_ref[1]
    own = rows_ref.shape[0]
    rows_ref[...] = basis_ref[pl.ds(pl.multiple_of(me * own, own), own), :]

    def late_moves(r, carry):
        rows = pl.ds(pl.multiple_of(r * 256, 256), 256)
        moved_ref[rows, late] = mm(mixed_ref[rows, :], basis_ref[:, late], ((1,), (0,))).astype(BF16)
        return carry

    def rotate(r, carry):
        rows = pl.ds(pl.multiple_of(r * 256, 256), 256)
        mine = basis_ref[:, rows]
        for ref, side in ((give_ref, 1 - core), (keep_ref, core)):
            cols = moved_ref[:, pl.ds(pl.multiple_of(side * half, half), half)]
            ref[rows, :] = (mm(mine, cols, ((0,), (0,))) * (1.0 / n)).astype(BF16)
        return carry

    lax.fori_loop(0, n // 256, late_moves, 0)
    lax.fori_loop(0, n // 256, rotate, 0)


VMEM = pl.BlockSpec(memory_space=pltpu.VMEM)
SMEM = pl.BlockSpec(memory_space=pltpu.SMEM)
HBM = pl.BlockSpec(memory_space=pltpu.HBM)


def basis_and_rotation(x1, x2, mixed, place, own):
    n, half = x1.shape
    sds = jax.ShapeDtypeStruct
    tall, square = sds((n, half), BF16), sds((half, half), BF16)
    pair, strip = sds((n, 2 * NB), BF16), sds((half, NB), F32)
    params = pltpu.CompilerParams(vmem_limit_bytes=60 * 2**20)
    a, wp = pltpu.VMEM((half, half), F32), pltpu.VMEM((2 * NB, 2 * NB), BF16)
    out = [square, square, square, pair, pair, strip]
    uh, um, ul, bh, bm, w = pl.pallas_call(
        first_kernel,
        out_shape=out,
        in_specs=[VMEM],
        out_specs=[HBM] * len(out),
        scratch_shapes=[pltpu.VMEM(s.shape, s.dtype) for s in out]
        + [a, wp, wp, pltpu.VMEM((NB, NB), F32), pltpu.SemaphoreType.DMA((len(out),))],
        compiler_params=params,
    )(x1)
    operands = (x2, x1, w, uh, um, ul, bh, bm, mixed)
    waiting = operands[:6] + operands[8:]
    return pl.pallas_call(
        second_kernel,
        out_shape=[sds((own, n), BF16), tall, tall],
        in_specs=[SMEM] + [HBM] * len(operands),
        out_specs=[VMEM] * 3,
        scratch_shapes=[pltpu.VMEM(s.shape, s.dtype) for s in waiting]
        + [pltpu.VMEM((n, n), BF16), pltpu.VMEM((n, half), BF16), pltpu.VMEM((n, half), BF16)]
        + [pltpu.VMEM((half, half), BF16)] * 6
        + [wp, wp, pltpu.VMEM((half, NB), F32), a, pltpu.VMEM((n, half), F32)]
        + [pltpu.VMEM((n, n), BF16), pltpu.SemaphoreType.DMA((len(operands),))],
        compiler_params=params,
    )(place, *operands)


def sigma_kernel(
    coef_ref, dim_ref, psi_ref, left_hbm, right_hbm, sent_ref, denom_ref,
    app_ref, left_ref, right_ref, sems,
):
    n = psi_ref.shape[0]
    step = 256
    count = left_ref.shape[0]
    pairs = range(count)
    dim = dim_ref[0]
    part = n // 2

    def fetch(at, i):
        source, held = (left_hbm, left_ref) if at == 0 else (right_hbm, right_ref)
        rows = pl.ds((i % 2) * part, part)
        return pltpu.make_async_copy(source.at[0, i // 2, rows, :], held.at[i // 2, rows, :], sems.at[at, i])

    queue = [fetch(at, i) for at in (0, 1) for i in range(2 * count)]
    for copy in queue[:2]:
        copy.start()

    def apply(i, carry):
        fetch(0, i).wait()
        for j in range(2 * count):
            following = queue[2 + 2 * j : 4 + 2 * j]

            @pl.when(i == j)
            def _():
                for copy in following:
                    copy.start()

        rows = pl.ds(pl.multiple_of((i % 2) * part, part), part)
        app_ref[i // 2, rows, :] = mm(left_ref[i // 2, rows, :], psi_ref[...], ((1,), (0,))).astype(BF16)
        return carry

    lax.fori_loop(0, 2 * count, apply, 0)
    for copy in queue[2 * count :]:
        copy.wait()
    row = lax.broadcasted_iota(jnp.int32, (n, step), 0)

    def columns(c, sums):
        cols = pl.ds(pl.multiple_of(c * step, step), step)
        total = coef_ref[0] * mm(app_ref[0], right_ref[0, cols, :], ((1,), (1,)))
        for p in pairs[1:]:
            total = total + coef_ref[p] * mm(app_ref[p], right_ref[p, cols, :], ((1,), (1,)))
        col = lax.broadcasted_iota(jnp.int32, (n, step), 1) + c * step
        total = jnp.where((row < dim) & (col < dim), total, F32(0))
        psi = psi_ref[:, cols].astype(F32)
        sent_ref[:, cols] = total.astype(BF16)
        return sums[0] + jnp.sum(psi * total), sums[1] + jnp.sum(psi * psi)

    numer, denom = lax.fori_loop(0, n // step, columns, (F32(0), F32(0)))
    lane = lax.broadcasted_iota(jnp.int32, (n, NB), 1)
    numer = jnp.full((n, NB), numer, F32)
    high, mid, low = (part.astype(F32) for part in three(numer))
    tail = jnp.where(lane == 0, high, jnp.where(lane == 1, mid, jnp.where(lane == 2, low, F32(0))))
    sent_ref[:, n:] = tail.astype(BF16)
    denom_ref[0] = denom


def sigma_part(coef, dim, psi, left_ops, right_ops):
    n = psi.shape[0]
    sds = jax.ShapeDtypeStruct
    return pl.pallas_call(
        sigma_kernel,
        out_shape=[sds((n, n + NB), BF16), sds((1,), F32)],
        in_specs=[SMEM, SMEM, VMEM, HBM, HBM],
        out_specs=[VMEM, SMEM],
        scratch_shapes=[pltpu.VMEM(left_ops.shape[1:], BF16)] * 3
        + [pltpu.SemaphoreType.DMA((2, 2 * left_ops.shape[1]))],
        compiler_params=pltpu.CompilerParams(vmem_limit_bytes=46 * 2**20),
    )(coef, dim, psi, left_ops, right_ops)


def from_everyone(x, axis):
    count = lax.axis_size(axis)
    return lax.all_to_all(jnp.broadcast_to(x[None], (count, *x.shape)), axis, 0, 0, tiled=True)


def rows_of_all(x):
    got = from_everyone(x, OPS)
    return got.reshape(-1, got.shape[-1])


def to_owners(x):
    tiles = x.reshape(lax.axis_size(OPS), -1, x.shape[-1])
    return lax.all_to_all(tiles, OPS, 0, 0, tiled=True).astype(F32)


def shards(wavefunction, diag_scale, sector_dims, left_ops, right_ops, weight_index, weight_table):
    psi_local = wavefunction[0]
    rows_dev, order_k = psi_local.shape
    half = order_k // 2
    me = lax.axis_index(OPS)
    dim = sector_dims[0]
    live = jnp.arange(order_k) < dim
    row_live = me * rows_dev + jnp.arange(rows_dev) < dim
    mine = jnp.where(row_live[:, None] & live[None, :], psi_local, BF16(0))
    psi = rows_of_all(mine)
    onehot = weight_index[0][:, None] == jnp.arange(weight_table.shape[0])[None, :]
    coef = jnp.sum(jnp.where(onehot, weight_table[None, :], F32(0)), axis=1)
    mixed = coef[0] * left_ops[0, 0].astype(F32)
    for p in range(1, left_ops.shape[1]):
        mixed = mixed + coef[p] * left_ops[0, p].astype(F32)
    psi, mixed = lax.optimization_barrier((psi, mixed.astype(BF16)))
    sent, denom = sigma_part(coef, sector_dims, psi, left_ops, right_ops)
    arrived = to_owners(sent)
    sigma = jnp.sum(arrived[:, :, :order_k], axis=0)
    energy = jnp.sum(arrived[:, 0, order_k:]) / denom[0]
    old = mine.astype(F32)
    update = (old + (sigma - energy * old) / diag_scale[0]).astype(BF16)
    x = [rows_of_all(update[:, h]) for h in (slice(0, half), slice(half, order_k))]
    core = lax.axis_index("sector") % 2
    place = jnp.stack([me, core]).astype(jnp.int32)
    basis_local, give, keep = basis_and_rotation(*x, mixed, place, rows_dev)

    def swapped(values, bits):
        count = lax.axis_size("sector")
        return lax.ppermute(values, "sector", [(i, i ^ bits) for i in range(count)])

    kept = (keep.astype(F32) + swapped(give, 1).astype(F32)).astype(BF16)
    owned = jnp.sum(to_owners(kept), axis=0).astype(BF16)
    near, far, cross = (swapped(owned, bits).astype(F32) for bits in (1, 2, 3))
    own, other = owned.astype(F32) + far, near + cross
    next_rows = jnp.concatenate(
        [jnp.where(core == 0, own, other), jnp.where(core == 0, other, own)], axis=1
    )
    return (basis_local[None], jnp.reshape(energy, (1,)), next_rows)


def solution(mesh):
    split = Mesh(
        mesh.devices.reshape(mesh.shape["sector"], 4, 4, 2), ("sector", "ops_0", "ops_1", "ops_2")
    )
    in_specs = (
        P("sector", OPS, None),
        P("sector", OPS, None),
        P("sector"),
        P("sector", OPS, None, None),
        P("sector", OPS, None, None),
        P("sector", OPS),
        P(),
    )
    out_specs = (P("sector", OPS, None), P("sector"), P(OPS, None))
    return jax.shard_map(
        shards, mesh=split, in_specs=in_specs, out_specs=out_specs, check_vma=False
    )
```
